32 devices in a mesh: dp: 8 (over y, x, core), tensor: 4 (over z).
Axes of the slice: x: 2, y: 2, z: 4, core: 2. Of those that a mesh axis runs over, the one named last changes fastest.
Arguments:
- gradient: bfloat16 [8, 256, 28672], P('dp', None, 'tensor'), may hold values from -6 to 6
- feedback: float32 [8, 256, 28672], P('dp', None, 'tensor'), may hold values from -4 to 4
- right_factor: float32 [28672, 32], P('tensor'), may hold values from -6 to 6
Outputs:
- new_feedback: float32 [8, 256, 28672], P('dp', None, 'tensor')
- left_factor: float32 [256, 32], replicated
- new_right: float32 [28672, 32], P('tensor')
The draws below stay inside these ranges and needn't reach their ends.
All inputs are finite; a program needn't handle non-finite values.
Results may differ from the reference program's by a relative error of at most 0.0003.
Values sent between devices are 32-bit elements; how exact they have to be, the bound alone decides.
No kernel may reach another device: no remote copies, remote signals or barrier semaphores. Data moves between devices by JAX's collectives and lax.ppermute only.
A program may use at most 64 MiB of HBM per device.

```python
import jax
import jax.numpy as jnp
from jax import lax

FF = 28672
RANK = 32
ROWS = 256
REPLICAS = 8
N_DP = 8


def steps_of(key, extent, cuts, least, largest):
    factor_of = 1.0
    for dim, shards_of in cuts:
        heights = jax.random.uniform(jax.random.fold_in(jax.random.fold_in(key, 6), dim), (shards_of,), jnp.float32, least / len(cuts), largest / len(cuts))
        factor_of = factor_of * jnp.repeat(jnp.exp(heights), extent[dim] // shards_of).reshape((-1,) + (1,) * (len(extent) - 1 - dim))
    return factor_of


def gaussian(rng, shape, width, reach, split=(), dtype=jnp.bfloat16):
    values = jax.random.normal(rng, shape, jnp.float32) * width
    if len(split) > 0:
        values = steps_of(rng, shape, split, -0.22, 0.18) * values
    return jnp.clip(values, min=-reach, max=reach).astype(dtype)


def setup_inputs(seed: int = 0) -> dict:
    streams_of = jax.random.split(jax.random.key(seed), 4)
    gradient = gaussian(streams_of[0], (REPLICAS, ROWS, FF), 1.0, 6.0, ((0, 8), (2, 4)))
    feedback = gaussian(streams_of[1], (REPLICAS, ROWS, FF), 0.5, 4.0, ((0, 8), (2, 4)), jnp.float32)
    right_factor = gaussian(streams_of[2], (FF, RANK), 1.0, 6.0, ((0, 4),), jnp.float32)
    return dict(gradient=gradient, feedback=feedback, right_factor=right_factor)


def orthonormal(matrix):
    gram_matrix = jnp.dot(matrix.T.astype(jnp.float32), matrix.astype(jnp.float32), precision=lax.Precision.HIGHEST, preferred_element_type=jnp.float32)
    lower = jnp.linalg.cholesky(gram_matrix)
    return lax.linalg.triangular_solve(lower, matrix, left_side=False, lower=True, transpose_a=True)

def reference(gradient, feedback, right_factor):
    combined = gradient.astype(jnp.float32) + feedback
    left_sum = jnp.einsum('drc,ck->rk', combined, right_factor, precision=lax.Precision.HIGHEST) / N_DP
    left_factor = orthonormal(left_sum)
    new_right = jnp.einsum('drc,rk->ck', combined, left_factor, precision=lax.Precision.HIGHEST) / N_DP
    approx = jnp.einsum('rk,ck->rc', left_factor, new_right, precision=lax.Precision.HIGHEST)
    new_feedback = combined - approx[None]
    return (new_feedback, left_factor, new_right)
```

```python
import jax
import jax.numpy as jnp
from jax import lax
from jax.sharding import PartitionSpec as P

HIGH = lax.Precision.HIGH
HIGHEST = lax.Precision.HIGHEST


def swap(x, axis, mask):
    size = lax.axis_size(axis)
    return lax.ppermute(x, axis, [(i, i ^ mask) for i in range(size)])


def tree(terms):
    while len(terms) > 1:
        terms = [a + b for a, b in zip(terms[::2], terms[1::2])]
    return terms[0]


def sum_over(x, axis, low, high):
    while low < high:
        step = min(2, high - low)
        x = tree([x] + [swap(x, axis, k << low) for k in range(1, 1 << step)])
        low += step
    return x


def bits(axis):
    size = lax.axis_size(axis)
    assert size & (size - 1) == 0
    return size.bit_length() - 1


def pick(x, index):
    return lax.dynamic_index_in_dim(x, index, 0, keepdims=False)


def per_device(gradient, feedback, right_factor):
    combined = gradient[0].astype(jnp.float32) + feedback[0]
    rows, columns = combined.shape
    rank = right_factor.shape[1]
    replicas = lax.axis_size("dp")
    me = lax.axis_index("dp")
    core, chip = me % 2, me // 2
    chips = replicas // 2

    left = jnp.dot(combined, right_factor, precision=HIGH, preferred_element_type=jnp.float32)
    left = sum_over(left, "dp", 0, 1)
    left = sum_over(left, "dp", 1, bits("dp"))
    left = sum_over(left, "tensor", 0, bits("tensor")) / replicas

    right = lax.dot_general(
        left, combined, (((0,), (0,)), ((), ())), precision=HIGH, preferred_element_type=jnp.float32
    )
    pieces = right.reshape(rank, 2, chips, columns // replicas).transpose(1, 2, 0, 3)
    half = pick(pieces, core) + swap(pick(pieces, 1 - core), "dp", 1)
    own = tree([pick(half, chip)] + [swap(pick(half, chip ^ k), "dp", 2 * k) for k in range(1, chips)])

    gram = lax.dot_general(
        left, left, (((0,), (0,)), ((), ())), precision=HIGHEST, preferred_element_type=jnp.float32
    )
    lower = jnp.linalg.cholesky(gram)
    inverse = lax.linalg.triangular_solve(lower, jnp.eye(rank, dtype=jnp.float32), left_side=True, lower=True)
    left_factor = lax.dot_general(
        left, inverse, (((1,), (1,)), ((), ())), precision=HIGHEST, preferred_element_type=jnp.float32
    )
    own = jnp.dot(inverse, own, precision=HIGHEST, preferred_element_type=jnp.float32) / replicas

    got = jnp.stack([own] + [swap(own, "dp", 2 * k) for k in range(1, chips)])
    mine = jnp.stack([pick(got, chip ^ k) for k in range(chips)])
    other = swap(mine, "dp", 1)
    both = jnp.stack([jnp.where(core == 0, mine, other), jnp.where(core == 0, other, mine)])
    new_right = both.transpose(2, 0, 1, 3).reshape(rank, columns)
    approx = jnp.dot(left_factor, new_right, precision=HIGH, preferred_element_type=jnp.float32)
    return ((combined - approx)[None], left_factor, new_right.T)


def solution(mesh):
    return jax.shard_map(
        per_device,
        mesh=mesh,
        in_specs=(P("dp", None, "tensor"), P("dp", None, "tensor"), P("tensor", None)),
        out_specs=(P("dp", None, "tensor"), P(), P("tensor", None)),
        check_vma=False,
    )
```

```python
import functools

import jax
import jax.numpy as jnp
from jax import lax
from jax.experimental import pallas as pl
from jax.experimental.pallas import tpu as pltpu
from jax.sharding import PartitionSpec as P

F32, BF16 = jnp.float32, jnp.bfloat16
HIGHEST = lax.Precision.HIGHEST
ANY = pl.BlockSpec(memory_space=pl.ANY)
VMEM = pl.BlockSpec(memory_space=pltpu.VMEM)


def split(x):
    high = x.astype(BF16)
    return high, (x - high.astype(F32)).astype(BF16)


def dot(a, b, a_dim, b_dim, precision=None):
    return lax.dot_general(a, b, (((a_dim,), (b_dim,)), ((), ())), precision=precision, preferred_element_type=F32)


def params(mebibytes):
    return pltpu.CompilerParams(vmem_limit_bytes=mebibytes << 20)


def cost(flops, bytes_accessed):
    return pl.CostEstimate(flops=int(flops), bytes_accessed=int(bytes_accessed), transcendentals=0)


def left_kernel(chunk, gradient, feedback, right, combined, high, low, left, gradient_buf, right_buf, sems):
    rows, columns = gradient.shape
    rank = right.shape[0]
    blocks = [pl.ds(i * chunk, chunk) for i in range(columns // chunk)]
    copies = []
    for i, at in enumerate(blocks):
        group = [
            pltpu.make_async_copy(gradient.at[:, at], gradient_buf.at[:, at], sems.at[0, i]),
            pltpu.make_async_copy(feedback.at[:, at], combined.at[:, at], sems.at[1, i]),
            pltpu.make_async_copy(right.at[:, at], right_buf.at[:, at], sems.at[2, i]),
        ]
        for copy in group:
            copy.start()
        copies.append(group)
    padded = combined.shape[1]
    if padded > columns:
        rest = pl.ds(columns, padded - columns)
        combined[:, rest] = jnp.zeros((rows, padded - columns), F32)
        high[:, rest] = jnp.zeros((rows, padded - columns), BF16)
        low[:, rest] = jnp.zeros((rows, padded - columns), BF16)
    total = jnp.zeros((rows, 2 * rank), F32)
    for at, group in zip(blocks, copies):
        for copy in group:
            copy.wait()
        both = jnp.concatenate(split(right_buf[:, at]), axis=0)
        c = combined[:, at] + gradient_buf[:, at].astype(F32)
        c_high, c_low = split(c)
        combined[:, at] = c
        high[:, at] = c_high
        low[:, at] = c_low
        total += dot(c_high, both, 1, 1) + dot(c_low, both, 1, 1)
    left[...] = (total[:, :rank] + total[:, rank:]).T


def left_product(gradient, feedback, right, padded):
    rows, columns = gradient.shape
    rank = right.shape[0]
    chunk = 512 if columns % 512 == 0 else 128
    return pl.pallas_call(
        functools.partial(left_kernel, chunk),
        in_specs=[ANY] * 3,
        out_specs=[VMEM] * 4,
        out_shape=[
            pltpu.VMEM((rows, padded), F32),
            pltpu.VMEM((rows, padded), BF16),
            pltpu.VMEM((rows, padded), BF16),
            pltpu.VMEM((rank, rows), F32),
        ],
        scratch_shapes=[
            pltpu.VMEM((rows, columns), BF16),
            pltpu.VMEM((rank, columns), F32),
            pltpu.SemaphoreType.DMA((3, columns // chunk)),
        ],
        compiler_params=params(16),
        cost_estimate=cost(8 * rows * columns * rank, 6 * rows * columns),
        name="left",
    )(gradient, feedback, right)


def right_kernel(index, left, high, low, pieces):
    chips, rank, width = pieces.shape
    half = chips * width
    block = 512 if half % 512 == 0 else 128
    both = jnp.concatenate(split(left[...]), axis=0)
    for i in range(half // block):
        at = pl.ds(pl.multiple_of(index[0] * half + i * block, block), block)
        total = dot(both, high[:, at], 1, 0) + dot(both, low[:, at], 1, 0)
        total = total[:rank] + total[rank:]
        start = i * block
        while start < (i + 1) * block:
            piece = start // width
            stop = min((i + 1) * block, (piece + 1) * width)
            pieces[piece, :, start - piece * width : stop - piece * width] = total[:, start - i * block : stop - i * block]
            start = stop


def right_product(index, left, high, low, chips, width):
    rank, rows = left.shape
    return pl.pallas_call(
        right_kernel,
        in_specs=[pl.BlockSpec(memory_space=pltpu.SMEM)] + [VMEM] * 3,
        out_specs=VMEM,
        out_shape=pltpu.VMEM((chips, rank, width), F32),
        compiler_params=params(8),
        cost_estimate=cost(8 * rows * chips * width * rank, 4 * rows * chips * width),
        name="right",
    )(index.reshape(1), left, high, low)


def factor_kernel(left, inverse, factor, stacked):
    rank, rows = left.shape
    values = left[...]
    gram = dot(values, values, 1, 1, HIGHEST)
    row = lax.broadcasted_iota(jnp.int32, (rank, rank), 0)
    column = lax.broadcasted_iota(jnp.int32, (rank, rank), 1)
    unit = (row == column).astype(F32)
    wide = jnp.concatenate([gram, unit], axis=1)
    row_of = lax.broadcasted_iota(jnp.int32, (rank, 1), 0)
    for j in range(rank - 1):
        pivot = wide[j : j + 1, :]
        scaled = pivot * (1.0 / pivot[:, j : j + 1])
        wide = wide - jnp.where(row_of > j, wide[:, j : j + 1], 0.0) * scaled
    diagonal = jnp.sum(wide[:, :rank] * unit, axis=1, keepdims=True)
    inv = wide[:, rank:] * (1.0 / jnp.sqrt(diagonal))
    inverse[...] = inv
    q = dot(inv, values, 1, 0, HIGHEST)
    factor[...] = q
    q_high, q_low = (part.astype(F32) for part in split(q))
    stacked[...] = jnp.concatenate([q_high, q_low, q_high, q_low], axis=0).T.astype(BF16)


def factors(left):
    rank, rows = left.shape
    return pl.pallas_call(
        factor_kernel,
        in_specs=[VMEM],
        out_specs=[VMEM] * 3,
        out_shape=[
            pltpu.VMEM((rank, rank), F32),
            pltpu.VMEM((rank, rows), F32),
            pltpu.VMEM((rows, 4 * rank), BF16),
        ],
        compiler_params=params(8),
        cost_estimate=cost(2e9, 1e6),
        name="factor",
    )(left)


def feedback_kernel(aliased, columns, index, stacked, pieces, combined, *refs):
    feedback, right, feedback_buf, sems = refs[2 * aliased :]
    rank = pieces[0].shape[-2]
    chips, rows, width = feedback_buf.shape
    whole = combined.shape[1] == columns
    copies = []
    for k in range(chips):
        place = index[0] * chips + (index[1] ^ k)
        at = pl.ds(pl.multiple_of(place * width, 128), width)
        piece = pieces[k]
        piece_high, piece_low = split(piece[...])
        four = jnp.concatenate([piece_high, piece_high, piece_low, piece_low], axis=0)
        feedback_buf[k] = combined[:, at] - dot(stacked[...], four, 1, 0)
        copies.append(
            (
                place * width < columns,
                pltpu.make_async_copy(feedback_buf.at[k], feedback.at[:, at], sems.at[0, k]),
                pltpu.make_async_copy(piece, right.at[:, at], sems.at[1, k]),
            )
        )
        start_or_wait(copies[-1], whole, "start")
    for copy in copies:
        start_or_wait(copy, whole, "wait")


def start_or_wait(copy, whole, action):
    inside, *both = copy

    def run():
        for one in both:
            getattr(one, action)()

    if whole:
        run()
    else:
        pl.when(inside)(run)


def new_feedback(index, stacked, pieces, combined, columns, before=()):
    rows = combined.shape[0]
    separate = isinstance(pieces, list)
    chips = len(pieces) if separate else pieces.shape[0]
    rank, width = (pieces[0] if separate else pieces).shape[-2:]
    given = pieces if separate else [pieces]

    def kernel(index, stacked, *refs):
        mine = refs[: len(given)]
        parts = list(mine) if separate else [mine[0].at[k] for k in range(chips)]
        feedback_kernel(len(before) // 2, columns, index, stacked, parts, *refs[len(given) :])

    return pl.pallas_call(
        kernel,
        in_specs=[pl.BlockSpec(memory_space=pltpu.SMEM)] + [VMEM] * (2 + len(given)) + [ANY] * len(before),
        out_specs=[ANY] * 2,
        out_shape=[jax.ShapeDtypeStruct((rows, columns), F32), jax.ShapeDtypeStruct((rank, columns), F32)],
        input_output_aliases={3 + len(given) + i: i for i in range(len(before))},
        scratch_shapes=[
            pltpu.VMEM((chips, rows, width), F32),
            pltpu.SemaphoreType.DMA((2, chips)),
        ],
        compiler_params=params(16),
        cost_estimate=cost(8 * rows * chips * width * rank, 4 * rows * chips * width),
        name="feedback",
    )(index, stacked, *given, combined, *before)


def swap(x, axis, mask):
    size = lax.axis_size(axis)
    return lax.ppermute(x, axis, [(i, i ^ mask) for i in range(size)])


def tree(terms):
    while len(terms) > 1:
        terms = [a + b for a, b in zip(terms[::2], terms[1::2])]
    return terms[0]


def sum_over(x, axis, low, high):
    while low < high:
        step = min(2, high - low)
        x = tree([x] + [swap(x, axis, k << low) for k in range(1, 1 << step)])
        low += step
    return x


def bits(axis):
    size = lax.axis_size(axis)
    assert size & (size - 1) == 0
    return size.bit_length() - 1


def pick(x, index):
    return lax.dynamic_index_in_dim(x, index, 0, keepdims=False)


def per_device(gradient, feedback, right_factor):
    gradient, feedback = gradient[0], feedback[0]
    columns = gradient.shape[1]
    replicas = lax.axis_size("dp")
    me = lax.axis_index("dp")
    core, chip = me % 2, me // 2
    chips = replicas // 2
    width = -(-columns // (replicas * 128)) * 128
    assert columns % width == 0

    combined, high, low, left = left_product(gradient, feedback, right_factor.T, replicas * width)
    left = sum_over(left, "dp", 0, 1)
    left = sum_over(left, "dp", 1, bits("dp"))
    left = sum_over(left, "tensor", 0, bits("tensor")) / replicas

    theirs = swap(right_product(1 - core, left, high, low, chips, width), "dp", 1)
    half = right_product(core, left, high, low, chips, width) + theirs
    own = tree([pick(half, chip)] + [swap(pick(half, chip ^ k), "dp", 2 * k) for k in range(1, chips)])

    inverse, factor, stacked = factors(left)
    own = jnp.dot(inverse, own, precision=HIGHEST, preferred_element_type=F32) / replicas

    got = [own] + [swap(own, "dp", 2 * k) for k in range(1, chips)]
    other = swap(jnp.stack(got), "dp", 1)
    place = jnp.stack([core, chip])
    outs = new_feedback(place, stacked, got, combined, columns)
    place = jnp.stack([1 - core, chip])
    outs = new_feedback(place, stacked, other, combined, columns, tuple(outs))
    return (outs[0][None], factor.T, outs[1].T)


def solution(mesh):
    return jax.shard_map(
        per_device,
        mesh=mesh,
        in_specs=(P("dp", None, "tensor"), P("dp", None, "tensor"), P("tensor", None)),
        out_specs=(P("dp", None, "tensor"), P(), P("tensor", None)),
        check_vma=False,
    )
```

```python
import functools

import jax
import jax.numpy as jnp
from jax import lax
from jax.experimental import pallas as pl
from jax.experimental.pallas import tpu as pltpu
from jax.sharding import PartitionSpec as P

F32, BF16 = jnp.float32, jnp.bfloat16
HIGHEST = lax.Precision.HIGHEST
ANY = pl.BlockSpec(memory_space=pl.ANY)
VMEM = pl.BlockSpec(memory_space=pltpu.VMEM)


def split(x):
    high = x.astype(BF16)
    return high, (x - high.astype(F32)).astype(BF16)


def dot(a, b, a_dim, b_dim, precision=None):
    return lax.dot_general(a, b, (((a_dim,), (b_dim,)), ((), ())), precision=precision, preferred_element_type=F32)


def keep(x, space):
    return pltpu.with_memory_space_constraint(x, space)


def position():
    me = lax.axis_index("dp")
    return lax.rem(me, 2), lax.div(me, 2)


def params(mebibytes):
    return pltpu.CompilerParams(vmem_limit_bytes=mebibytes << 20)


def cost(flops, bytes_accessed):
    return pl.CostEstimate(flops=int(flops), bytes_accessed=int(bytes_accessed), transcendentals=0)


def left_kernel(chunk, gradient, feedback, right, combined, high, low, left, gradient_buf, right_buf, sems):
    rows, columns = gradient.shape
    rank = right.shape[0]
    blocks = [pl.ds(i * chunk, chunk) for i in range(columns // chunk)]
    copies = []
    for i, at in enumerate(blocks):
        group = [
            pltpu.make_async_copy(gradient.at[:, at], gradient_buf.at[:, at], sems.at[0, i]),
            pltpu.make_async_copy(feedback.at[:, at], combined.at[:, at], sems.at[1, i]),
            pltpu.make_async_copy(right.at[:, at], right_buf.at[:, at], sems.at[2, i]),
        ]
        for copy in group:
            copy.start()
        copies.append(group)
    padded = combined.shape[1]
    if padded > columns:
        rest = pl.ds(columns, padded - columns)
        combined[:, rest] = jnp.zeros((rows, padded - columns), F32)
        high[:, rest] = jnp.zeros((rows, padded - columns), BF16)
        low[:, rest] = jnp.zeros((rows, padded - columns), BF16)
    total = jnp.zeros((rows, 2 * rank), F32)
    for at, group in zip(blocks, copies):
        for copy in group:
            copy.wait()
        both = jnp.concatenate(split(right_buf[:, at]), axis=0)
        c = combined[:, at] + gradient_buf[:, at].astype(F32)
        c_high, c_low = split(c)
        combined[:, at] = c
        high[:, at] = c_high
        low[:, at] = c_low
        total += dot(c_high, both, 1, 1) + dot(c_low, both, 1, 1)
    left[...] = (total[:, :rank] + total[:, rank:]).T


def left_product(gradient, feedback, right, padded):
    rows, columns = gradient.shape
    rank = right.shape[0]
    chunk = 512 if columns % 512 == 0 else 128
    return pl.pallas_call(
        functools.partial(left_kernel, chunk),
        in_specs=[ANY] * 3,
        out_specs=[VMEM] * 4,
        out_shape=[
            pltpu.VMEM((rows, padded), F32),
            pltpu.VMEM((rows, padded), BF16),
            pltpu.VMEM((rows, padded), BF16),
            pltpu.VMEM((rank, rows), F32),
        ],
        scratch_shapes=[
            pltpu.VMEM((rows, columns), BF16),
            pltpu.VMEM((rank, columns), F32),
            pltpu.SemaphoreType.DMA((3, columns // chunk)),
        ],
        compiler_params=params(16),
        cost_estimate=cost(8 * rows * columns * rank, 6 * rows * columns),
        name="left",
    )(gradient, feedback, right)


def right_kernel(own, left, high, low, pieces):
    chips, rank, width = pieces.shape
    half = chips * width
    core, _ = position()
    side = core if own else 1 - core
    block = 512 if half % 512 == 0 else 128
    both = jnp.concatenate(split(left[...]), axis=0)
    for i in range(half // block):
        at = pl.ds(pl.multiple_of(side * half + i * block, block), block)
        total = dot(both, high[:, at], 1, 0) + dot(both, low[:, at], 1, 0)
        total = total[:rank] + total[rank:]
        start = i * block
        while start < (i + 1) * block:
            piece = start // width
            stop = min((i + 1) * block, (piece + 1) * width)
            pieces[piece, :, start - piece * width : stop - piece * width] = total[:, start - i * block : stop - i * block]
            start = stop


def right_product(own, left, high, low, chips, width):
    rank, rows = left.shape
    return pl.pallas_call(
        functools.partial(right_kernel, own),
        in_specs=[VMEM] * 3,
        out_specs=VMEM,
        out_shape=pltpu.VMEM((chips, rank, width), F32),
        compiler_params=params(8),
        cost_estimate=cost(8 * rows * chips * width * rank, 4 * rows * chips * width),
        name="right",
    )(left, high, low)


def share_kernel(a, b, *outs):
    _, chip = position()
    for k, out in enumerate(outs):
        out[...] = a[chip ^ k] + b[chip ^ k]


def share(a, b):
    chips, rank, width = a.shape
    return pl.pallas_call(
        share_kernel,
        in_specs=[VMEM] * 2,
        out_specs=[VMEM] * chips,
        out_shape=[pltpu.VMEM((rank, width), F32)] * chips,
        compiler_params=params(8),
        cost_estimate=cost(chips * rank * width, 12 * chips * rank * width),
        name="share",
    )(a, b)


def factor_kernel(left, inverse, factor, stacked):
    rank, rows = left.shape
    values = left[...]
    gram = dot(values, values, 1, 1, HIGHEST)
    row = lax.broadcasted_iota(jnp.int32, (rank, rank), 0)
    column = lax.broadcasted_iota(jnp.int32, (rank, rank), 1)
    unit = (row == column).astype(F32)
    wide = jnp.concatenate([gram, unit], axis=1)
    row_of = lax.broadcasted_iota(jnp.int32, (rank, 1), 0)
    for j in range(rank - 1):
        pivot = wide[j : j + 1, :]
        scaled = pivot * (1.0 / pivot[:, j : j + 1])
        wide = wide - jnp.where(row_of > j, wide[:, j : j + 1], 0.0) * scaled
    diagonal = jnp.sum(wide[:, :rank] * unit, axis=1, keepdims=True)
    inv = wide[:, rank:] * (1.0 / jnp.sqrt(diagonal))
    inverse[...] = inv
    q = dot(inv, values, 1, 0, HIGHEST)
    factor[...] = q
    q_high, q_low = (part.astype(F32) for part in split(q))
    stacked[...] = jnp.concatenate([q_high, q_low, q_high, q_low], axis=0).T.astype(BF16)


def factors(left):
    rank, rows = left.shape
    return pl.pallas_call(
        factor_kernel,
        in_specs=[VMEM],
        out_specs=[VMEM] * 3,
        out_shape=[
            pltpu.VMEM((rank, rank), F32),
            pltpu.VMEM((rank, rows), F32),
            pltpu.VMEM((rows, 4 * rank), BF16),
        ],
        compiler_params=params(8),
        cost_estimate=cost(2e9, 1e6),
        name="factor",
    )(left)


def feedback_kernel(own, aliased, columns, stacked, pieces, combined, *refs):
    feedback, right, feedback_buf, sems = refs[2 * aliased :]
    rank = pieces[0].shape[-2]
    chips, rows, width = feedback_buf.shape
    whole = combined.shape[1] == columns
    core, chip = position()
    side = core if own else 1 - core
    copies = []
    for k in range(chips):
        place = side * chips + (chip ^ k)
        at = pl.ds(pl.multiple_of(place * width, 128), width)
        piece = pieces[k]
        piece_high, piece_low = split(piece[...])
        four = jnp.concatenate([piece_high, piece_high, piece_low, piece_low], axis=0)
        feedback_buf[k] = combined[:, at] - dot(stacked[...], four, 1, 0)
        copies.append(
            (
                place * width < columns,
                pltpu.make_async_copy(feedback_buf.at[k], feedback.at[:, at], sems.at[0, k]),
                pltpu.make_async_copy(piece, right.at[:, at], sems.at[1, k]),
            )
        )
        start_or_wait(copies[-1], whole, "start")
    for copy in copies:
        start_or_wait(copy, whole, "wait")


def start_or_wait(copy, whole, action):
    inside, *both = copy

    def run():
        for one in both:
            getattr(one, action)()

    if whole:
        run()
    else:
        pl.when(inside)(run)


def new_feedback(own, stacked, pieces, combined, columns, before=()):
    rows = combined.shape[0]
    separate = isinstance(pieces, list)
    chips = len(pieces) if separate else pieces.shape[0]
    rank, width = (pieces[0] if separate else pieces).shape[-2:]
    given = pieces if separate else [pieces]

    def kernel(stacked, *refs):
        mine = refs[: len(given)]
        parts = list(mine) if separate else [mine[0].at[k] for k in range(chips)]
        feedback_kernel(own, len(before) // 2, columns, stacked, parts, *refs[len(given) :])

    return pl.pallas_call(
        kernel,
        in_specs=[VMEM] * (2 + len(given)) + [ANY] * len(before),
        out_specs=[ANY] * 2,
        out_shape=[jax.ShapeDtypeStruct((rows, columns), F32), jax.ShapeDtypeStruct((rank, columns), F32)],
        input_output_aliases={2 + len(given) + i: i for i in range(len(before))},
        scratch_shapes=[
            pltpu.VMEM((chips, rows, width), F32),
            pltpu.SemaphoreType.DMA((2, chips)),
        ],
        compiler_params=params(16),
        cost_estimate=cost(8 * rows * chips * width * rank, 4 * rows * chips * width),
        name="feedback",
    )(stacked, *given, combined, *before)


def swap(x, axis, mask):
    size = lax.axis_size(axis)
    return lax.ppermute(x, axis, [(i, i ^ mask) for i in range(size)])


def tree(terms):
    while len(terms) > 1:
        terms = [a + b for a, b in zip(terms[::2], terms[1::2])]
    return terms[0]


def sum_over(x, axis, low, high):
    while low < high:
        step = min(2, high - low)
        x = tree([x] + [swap(x, axis, k << low) for k in range(1, 1 << step)])
        low += step
    return x


def bits(axis):
    size = lax.axis_size(axis)
    assert size & (size - 1) == 0
    return size.bit_length() - 1


def per_device(gradient, feedback, right_factor):
    gradient, feedback = gradient[0], feedback[0]
    columns = gradient.shape[1]
    replicas = lax.axis_size("dp")
    chips = replicas // 2
    width = -(-columns // (replicas * 128)) * 128
    assert columns % width == 0

    given = [keep(x, pltpu.HBM) for x in (gradient, feedback, right_factor.T)]
    combined, high, low, left = left_product(*given, replicas * width)
    combined, high, low = (keep(x, pltpu.VMEM) for x in (combined, high, low))
    left = sum_over(left, "dp", 0, 1)
    left = sum_over(left, "dp", 1, bits("dp"))
    left = sum_over(left, "tensor", 0, bits("tensor")) / replicas

    theirs = swap(right_product(False, left, high, low, chips, width), "dp", 1)
    own, *away = share(right_product(True, left, high, low, chips, width), theirs)
    own = tree([own] + [swap(x, "dp", 2 * k) for k, x in enumerate(away, 1)])

    inverse, factor, stacked = factors(left)
    own = jnp.dot(inverse, own, precision=HIGHEST, preferred_element_type=F32) / replicas

    got = [own] + [swap(own, "dp", 2 * k) for k in range(1, chips)]
    other = swap(jnp.stack(got), "dp", 1)
    outs = new_feedback(True, stacked, got, combined, columns)
    outs = new_feedback(False, stacked, other, combined, columns, tuple(outs))
    return (outs[0][None], factor.T, outs[1].T)


def solution(mesh):
    return jax.shard_map(
        per_device,
        mesh=mesh,
        in_specs=(P("dp", None, "tensor"), P("dp", None, "tensor"), P("tensor", None)),
        out_specs=(P("dp", None, "tensor"), P(), P("tensor", None)),
        check_vma=False,
    )
```

```python
import functools

import jax
import jax.numpy as jnp
from jax import lax
from jax.experimental import pallas as pl
from jax.experimental.pallas import tpu as pltpu
from jax.sharding import PartitionSpec as P

F32, BF16 = jnp.float32, jnp.bfloat16
HIGHEST = lax.Precision.HIGHEST
ANY = pl.BlockSpec(memory_space=pl.ANY)
VMEM = pl.BlockSpec(memory_space=pltpu.VMEM)


def split(x):
    high = x.astype(BF16)
    return high, (x - high.astype(F32)).astype(BF16)


def dot(a, b, a_dim, b_dim, precision=None):
    return lax.dot_general(a, b, (((a_dim,), (b_dim,)), ((), ())), precision=precision, preferred_element_type=F32)


def keep(x, space):
    return pltpu.with_memory_space_constraint(x, space)


def position():
    me = lax.axis_index("dp")
    return lax.rem(me, 2), lax.div(me, 2)


def params(mebibytes):
    return pltpu.CompilerParams(vmem_limit_bytes=mebibytes << 20)


def cost(flops, bytes_accessed):
    return pl.CostEstimate(flops=int(flops), bytes_accessed=int(bytes_accessed), transcendentals=0)


def left_kernel(chunk, gradient, feedback, right, combined, high, low, left, gradient_buf, right_buf, sems):
    rows, columns = gradient.shape
    rank = right.shape[0]
    blocks = [pl.ds(i * chunk, chunk) for i in range(columns // chunk)]
    copies = []
    for i, at in enumerate(blocks):
        group = [
            pltpu.make_async_copy(gradient.at[:, at], gradient_buf.at[:, at], sems.at[0, i]),
            pltpu.make_async_copy(feedback.at[:, at], combined.at[:, at], sems.at[1, i]),
            pltpu.make_async_copy(right.at[:, at], right_buf.at[:, at], sems.at[2, i]),
        ]
        for copy in group:
            copy.start()
        copies.append(group)
    padded = combined.shape[1]
    if padded > columns:
        rest = pl.ds(columns, padded - columns)
        combined[:, rest] = jnp.zeros((rows, padded - columns), F32)
        high[:, rest] = jnp.zeros((rows, padded - columns), BF16)
        low[:, rest] = jnp.zeros((rows, padded - columns), BF16)
    total = jnp.zeros((rows, 2 * rank), F32)
    for at, group in zip(blocks, copies):
        for copy in group:
            copy.wait()
        both = jnp.concatenate(split(right_buf[:, at]), axis=0)
        c = combined[:, at] + gradient_buf[:, at].astype(F32)
        c_high, c_low = split(c)
        combined[:, at] = c
        high[:, at] = c_high
        low[:, at] = c_low
        total += dot(c_high, both, 1, 1) + dot(c_low, both, 1, 1)
    left[...] = (total[:, :rank] + total[:, rank:]).T


def left_product(gradient, feedback, right, padded):
    rows, columns = gradient.shape
    rank = right.shape[0]
    chunk = next(c for c in (1024, 512, 128) if columns % c == 0)
    return pl.pallas_call(
        functools.partial(left_kernel, chunk),
        in_specs=[ANY] * 3,
        out_specs=[VMEM] * 4,
        out_shape=[
            pltpu.VMEM((rows, padded), F32),
            pltpu.VMEM((rows, padded), BF16),
            pltpu.VMEM((rows, padded), BF16),
            pltpu.VMEM((rank, rows), F32),
        ],
        scratch_shapes=[
            pltpu.VMEM((rows, columns), BF16),
            pltpu.VMEM((rank, columns), F32),
            pltpu.SemaphoreType.DMA((3, columns // chunk)),
        ],
        compiler_params=params(16),
        cost_estimate=cost(8 * rows * columns * rank, 6 * rows * columns),
        name="left",
    )(gradient, feedback, right)


def right_kernel(own, left, high, low, pieces):
    chips, rank, width = pieces.shape
    half = chips * width
    core, _ = position()
    side = core if own else 1 - core
    block = 512 if half % 512 == 0 else 128
    both = jnp.concatenate(split(left[...]), axis=0)
    for i in range(half // block):
        at = pl.ds(pl.multiple_of(side * half + i * block, block), block)
        total = dot(both, high[:, at], 1, 0) + dot(both, low[:, at], 1, 0)
        total = total[:rank] + total[rank:]
        start = i * block
        while start < (i + 1) * block:
            piece = start // width
            stop = min((i + 1) * block, (piece + 1) * width)
            pieces[piece, :, start - piece * width : stop - piece * width] = total[:, start - i * block : stop - i * block]
            start = stop


def right_product(own, left, high, low, chips, width):
    rank, rows = left.shape
    return pl.pallas_call(
        functools.partial(right_kernel, own),
        in_specs=[VMEM] * 3,
        out_specs=VMEM,
        out_shape=pltpu.VMEM((chips, rank, width), F32),
        compiler_params=params(8),
        cost_estimate=cost(8 * rows * chips * width * rank, 4 * rows * chips * width),
        name="right",
    )(left, high, low)


def share_kernel(a, b, *outs):
    _, chip = position()
    for k, out in enumerate(outs):
        out[...] = a[chip ^ k] + b[chip ^ k]


def share(a, b):
    chips, rank, width = a.shape
    return pl.pallas_call(
        share_kernel,
        in_specs=[VMEM] * 2,
        out_specs=[VMEM] * chips,
        out_shape=[pltpu.VMEM((rank, width), F32)] * chips,
        compiler_params=params(8),
        cost_estimate=cost(chips * rank * width, 12 * chips * rank * width),
        name="share",
    )(a, b)


def factor_kernel(left, inverse, factor, stacked):
    rank, rows = left.shape
    values = left[...]
    gram = dot(values, values, 1, 1, HIGHEST)
    row = lax.broadcasted_iota(jnp.int32, (rank, rank), 0)
    column = lax.broadcasted_iota(jnp.int32, (rank, rank), 1)
    unit = (row == column).astype(F32)
    wide = jnp.concatenate([gram, unit], axis=1)
    row_of = lax.broadcasted_iota(jnp.int32, (rank, 1), 0)
    for j in range(rank - 1):
        pivot = wide[j : j + 1, :]
        scaled = pivot * (1.0 / pivot[:, j : j + 1])
        wide = wide - jnp.where(row_of > j, wide[:, j : j + 1], 0.0) * scaled
    diagonal = jnp.sum(wide[:, :rank] * unit, axis=1, keepdims=True)
    inv = wide[:, rank:] * (1.0 / jnp.sqrt(diagonal))
    inverse[...] = inv
    q = dot(inv, values, 1, 0, HIGHEST)
    factor[...] = q
    q_high, q_low = (part.astype(F32) for part in split(q))
    stacked[...] = jnp.concatenate([q_high, q_low, q_high, q_low], axis=0).T.astype(BF16)


def factors(left):
    rank, rows = left.shape
    return pl.pallas_call(
        factor_kernel,
        in_specs=[VMEM],
        out_specs=[VMEM] * 3,
        out_shape=[
            pltpu.VMEM((rank, rank), F32),
            pltpu.VMEM((rank, rows), F32),
            pltpu.VMEM((rows, 4 * rank), BF16),
        ],
        compiler_params=params(8),
        cost_estimate=cost(2e9, 1e6),
        name="factor",
    )(left)


def feedback_kernel(order, columns, stacked, pieces, combined, feedback, right, token, feedback_buf, sems):
    chips, width = combined.shape[1] // (2 * feedback_buf.shape[2]), feedback_buf.shape[2]
    core, chip = position()
    whole = combined.shape[1] == columns
    copies = []
    for i, (other, k) in enumerate(order):
        place = (1 - core if other else core) * chips + (chip ^ k)
        at = pl.ds(pl.multiple_of(place * width, 128), width)
        piece_high, piece_low = split(pieces[i][...])
        four = jnp.concatenate([piece_high, piece_high, piece_low, piece_low], axis=0)
        feedback_buf[i] = combined[:, at] - dot(stacked[...], four, 1, 0)
        copies.append(
            (
                place * width < columns,
                pltpu.make_async_copy(feedback_buf.at[i], feedback.at[:, at], sems.at[0, i]),
                pltpu.make_async_copy(pieces[i], right.at[:, at], sems.at[1, i]),
            )
        )
        start_or_wait(copies[-1], whole, "start")
    token[...] = jnp.zeros_like(token)
    for copy in copies:
        start_or_wait(copy, whole, "wait")


def start_or_wait(copy, whole, action):
    inside, *both = copy

    def run():
        for one in both:
            getattr(one, action)()

    if whole:
        run()
    else:
        pl.when(inside)(run)


def new_feedback(order, stacked, pieces, combined, columns, before):
    rows = combined.shape[0]
    separate = isinstance(pieces, list)
    given = pieces if separate else [pieces]
    count = len(order)
    rank, width = given[0].shape[-2:]

    def kernel(stacked, *refs):
        mine = refs[: len(given)]
        parts = list(mine) if separate else [mine[0].at[i] for i in range(count)]
        combined, *rest = refs[len(given) :]
        feedback_kernel(order, columns, stacked, parts, combined, *rest[len(before) :])

    return pl.pallas_call(
        kernel,
        in_specs=[VMEM] * (2 + len(given)) + [ANY] * len(before),
        out_specs=[ANY] * 2 + [VMEM],
        out_shape=[
            jax.ShapeDtypeStruct((rows, columns), F32),
            jax.ShapeDtypeStruct((rank, columns), F32),
            pltpu.VMEM((8, 128), F32),
        ],
        input_output_aliases={2 + len(given) + i: i for i in range(len(before))},
        scratch_shapes=[
            pltpu.VMEM((count, rows, width), F32),
            pltpu.SemaphoreType.DMA((2, count)),
        ],
        compiler_params=params(16),
        cost_estimate=cost(8 * rows * count * width * rank, 4 * rows * count * width),
        name="feedback",
    )(stacked, *given, combined, *before)


def swap(x, axis, mask):
    size = lax.axis_size(axis)
    return lax.ppermute(x, axis, [(i, i ^ mask) for i in range(size)])


def after(x, token):
    return lax.optimization_barrier((x, token))[0]


def tree(terms):
    while len(terms) > 1:
        terms = [a + b for a, b in zip(terms[::2], terms[1::2])]
    return terms[0]


def sum_over(x, axis, low, high):
    while low < high:
        step = min(2, high - low)
        came = [swap(x, axis, k << low) for k in reversed(range(1, 1 << step))]
        x = tree([x] + came[::-1])
        low += step
    return x


def bits(axis):
    size = lax.axis_size(axis)
    assert size & (size - 1) == 0
    return size.bit_length() - 1


def per_device(gradient, feedback, right_factor):
    gradient, feedback = gradient[0], feedback[0]
    columns = gradient.shape[1]
    replicas = lax.axis_size("dp")
    chips = replicas // 2
    width = -(-columns // (replicas * 128)) * 128
    assert columns % width == 0

    given = [keep(x, pltpu.HBM) for x in (gradient, feedback, right_factor.T)]
    combined, high, low, left = left_product(*given, replicas * width)
    combined, high, low = (keep(x, pltpu.VMEM) for x in (combined, high, low))
    left = sum_over(left, "dp", 0, 1)
    left = sum_over(left, "dp", 1, bits("dp"))
    left = sum_over(left, "tensor", 0, bits("tensor")) / replicas

    theirs = swap(right_product(False, left, high, low, chips, width), "dp", 1)
    own, *away = share(right_product(True, left, high, low, chips, width), theirs)
    came = [swap(x, "dp", 2 * k) for k, x in reversed(list(enumerate(away, 1)))]
    own = tree([own] + came[::-1])

    inverse, factor, stacked = factors(left)
    own = jnp.dot(inverse, own, precision=HIGHEST, preferred_element_type=F32) / replicas

    beside = swap(own, "dp", 1)
    far, near = [chips - 1], list(range(1, chips - 1))
    got = {k: swap(own, "dp", 2 * k) for k in far + near}
    update = functools.partial(new_feedback, stacked=stacked, combined=combined, columns=columns)
    *outs, token = update([(0, 0), (1, 0)], pieces=[own, beside], before=())
    got |= {k: after(got[k], token) for k in far}
    *outs, token = update([(0, k) for k in far], pieces=[got[k] for k in far], before=outs)
    got |= {k: after(got[k], token) for k in near}
    others = swap(jnp.stack([got[k] for k in far + near]), "dp", 1)
    *outs, _ = update([(0, k) for k in near], pieces=[got[k] for k in near], before=outs)
    *outs, _ = update([(1, k) for k in far + near], pieces=others, before=outs)
    return (outs[0][None], factor.T, outs[1].T)


def solution(mesh):
    return jax.shard_map(
        per_device,
        mesh=mesh,
        in_specs=(P("dp", None, "tensor"), P("dp", None, "tensor"), P("tensor", None)),
        out_specs=(P("dp", None, "tensor"), P(), P("tensor", None)),
        check_vma=False,
    )
```

```python
import functools

import jax
import jax.numpy as jnp
from jax import lax
from jax.experimental import pallas as pl
from jax.experimental.pallas import tpu as pltpu
from jax.sharding import PartitionSpec as P

F32, BF16 = jnp.float32, jnp.bfloat16
HIGHEST = lax.Precision.HIGHEST
ANY = pl.BlockSpec(memory_space=pl.ANY)
VMEM = pl.BlockSpec(memory_space=pltpu.VMEM)


def split(x):
    high = x.astype(BF16)
    return high, (x - high.astype(F32)).astype(BF16)


def dot(a, b, a_dim, b_dim, precision=None):
    return lax.dot_general(a, b, (((a_dim,), (b_dim,)), ((), ())), precision=precision, preferred_element_type=F32)


def keep(x, space):
    return pltpu.with_memory_space_constraint(x, space)


def position():
    me = lax.axis_index("dp")
    return lax.rem(me, 2), lax.div(me, 2)


def params(mebibytes):
    return pltpu.CompilerParams(vmem_limit_bytes=mebibytes << 20)


def cost(flops, bytes_accessed):
    return pl.CostEstimate(flops=int(flops), bytes_accessed=int(bytes_accessed), transcendentals=0)


def left_kernel(chunk, gradient, feedback, right, combined, high, low, left, gradient_buf, right_buf, sems):
    rows, columns = gradient.shape
    rank = right.shape[0]
    blocks = [pl.ds(i * chunk, chunk) for i in range(columns // chunk)]
    copies = []
    for i, at in enumerate(blocks):
        group = [
            pltpu.make_async_copy(gradient.at[:, at], gradient_buf.at[:, at], sems.at[0, i]),
            pltpu.make_async_copy(feedback.at[:, at], combined.at[:, at], sems.at[1, i]),
            pltpu.make_async_copy(right.at[:, at], right_buf.at[:, at], sems.at[2, i]),
        ]
        for copy in group:
            copy.start()
        copies.append(group)
    padded = combined.shape[1]
    if padded > columns:
        rest = pl.ds(columns, padded - columns)
        combined[:, rest] = jnp.zeros((rows, padded - columns), F32)
        high[:, rest] = jnp.zeros((rows, padded - columns), BF16)
        low[:, rest] = jnp.zeros((rows, padded - columns), BF16)
    total = jnp.zeros((rows, 2 * rank), F32)
    for at, group in zip(blocks, copies):
        for copy in group:
            copy.wait()
        both = jnp.concatenate(split(right_buf[:, at]), axis=0)
        c = combined[:, at] + gradient_buf[:, at].astype(F32)
        c_high, c_low = split(c)
        combined[:, at] = c
        high[:, at] = c_high
        low[:, at] = c_low
        total += dot(c_high, both, 1, 1) + dot(c_low, both, 1, 1)
    left[...] = (total[:, :rank] + total[:, rank:]).T


def left_product(gradient, feedback, right, padded):
    rows, columns = gradient.shape
    rank = right.shape[0]
    chunk = next(c for c in (1024, 512, 128) if columns % c == 0)
    return pl.pallas_call(
        functools.partial(left_kernel, chunk),
        in_specs=[ANY] * 3,
        out_specs=[VMEM] * 4,
        out_shape=[
            pltpu.VMEM((rows, padded), F32),
            pltpu.VMEM((rows, padded), BF16),
            pltpu.VMEM((rows, padded), BF16),
            pltpu.VMEM((rank, rows), F32),
        ],
        scratch_shapes=[
            pltpu.VMEM((rows, columns), BF16),
            pltpu.VMEM((rank, columns), F32),
            pltpu.SemaphoreType.DMA((3, columns // chunk)),
        ],
        compiler_params=params(16),
        cost_estimate=cost(8 * rows * columns * rank, 6 * rows * columns),
        name="left",
    )(gradient, feedback, right)


def right_kernel(own, left, high, low, *refs):
    *before, pieces = refs
    chips, rank, width = pieces.shape
    half = chips * width
    core, _ = position()
    side = core if own else 1 - core
    block = 512 if half % 512 == 0 else 128
    both = jnp.concatenate(split(left[...]), axis=0)
    for i in range(half // block):
        at = pl.ds(pl.multiple_of(side * half + i * block, block), block)
        total = dot(both, high[:, at], 1, 0) + dot(both, low[:, at], 1, 0)
        total = total[:rank] + total[rank:]
        start = i * block
        while start < (i + 1) * block:
            piece = start // width
            stop = min((i + 1) * block, (piece + 1) * width)
            there = (piece, slice(None), slice(start - piece * width, stop - piece * width))
            part = total[:, start - i * block : stop - i * block]
            pieces[there] = before[0][there] + part if before else part
            start = stop


def right_product(own, left, high, low, chips, width, *before):
    rank, rows = left.shape
    return pl.pallas_call(
        functools.partial(right_kernel, own),
        in_specs=[VMEM] * (3 + len(before)),
        out_specs=VMEM,
        out_shape=pltpu.VMEM((chips, rank, width), F32),
        compiler_params=params(8),
        cost_estimate=cost(8 * rows * chips * width * rank, 4 * rows * chips * width),
        name="right",
    )(left, high, low, *before)


def share_kernel(a, b, *outs):
    _, chip = position()
    for k, out in enumerate(outs):
        out[...] = a[chip ^ k] + b[chip ^ k]


def share(a, b):
    chips, rank, width = a.shape
    return pl.pallas_call(
        share_kernel,
        in_specs=[VMEM] * 2,
        out_specs=[VMEM] * chips,
        out_shape=[pltpu.VMEM((rank, width), F32)] * chips,
        compiler_params=params(8),
        cost_estimate=cost(chips * rank * width, 12 * chips * rank * width),
        name="share",
    )(a, b)


def factor_kernel(left, inverse, factor, stacked):
    rank, rows = left.shape
    values = left[...]
    gram = dot(values, values, 1, 1, HIGHEST)
    row = lax.broadcasted_iota(jnp.int32, (rank, rank), 0)
    column = lax.broadcasted_iota(jnp.int32, (rank, rank), 1)
    unit = (row == column).astype(F32)
    wide = jnp.concatenate([gram, unit], axis=1)
    row_of = lax.broadcasted_iota(jnp.int32, (rank, 1), 0)
    for j in range(rank - 1):
        pivot = wide[j : j + 1, :]
        scaled = pivot * (1.0 / pivot[:, j : j + 1])
        wide = wide - jnp.where(row_of > j, wide[:, j : j + 1], 0.0) * scaled
    diagonal = jnp.sum(wide[:, :rank] * unit, axis=1, keepdims=True)
    inv = wide[:, rank:] * (1.0 / jnp.sqrt(diagonal))
    inverse[...] = inv
    q = dot(inv, values, 1, 0, HIGHEST)
    factor[...] = q
    q_high, q_low = (part.astype(F32) for part in split(q))
    stacked[...] = jnp.concatenate([q_high, q_low, q_high, q_low], axis=0).T.astype(BF16)


def factors(left):
    rank, rows = left.shape
    return pl.pallas_call(
        factor_kernel,
        in_specs=[VMEM],
        out_specs=[VMEM] * 3,
        out_shape=[
            pltpu.VMEM((rank, rank), F32),
            pltpu.VMEM((rank, rows), F32),
            pltpu.VMEM((rows, 4 * rank), BF16),
        ],
        compiler_params=params(8),
        cost_estimate=cost(2e9, 1e6),
        name="factor",
    )(left)


def feedback_kernel(own, columns, stacked, pieces, combined, factor, feedback, right, factor_out, feedback_buf, sems, factor_sem):
    rank = pieces[0].shape[-2]
    chips, rows, width = feedback_buf.shape
    whole = combined.shape[1] == columns
    core, chip = position()
    side = core if own else 1 - core
    copies = []
    if own:
        factor_copy = pltpu.make_async_copy(factor, factor_out, factor_sem)
        factor_copy.start()
    for k in range(chips):
        place = side * chips + (chip ^ k)
        at = pl.ds(pl.multiple_of(place * width, 128), width)
        piece = pieces[k]
        piece_high, piece_low = split(piece[...])
        four = jnp.concatenate([piece_high, piece_high, piece_low, piece_low], axis=0)
        feedback_buf[k] = combined[:, at] - dot(stacked[...], four, 1, 0)
        copies.append(
            (
                place * width < columns,
                pltpu.make_async_copy(feedback_buf.at[k], feedback.at[:, at], sems.at[0, k]),
                pltpu.make_async_copy(piece, right.at[:, at], sems.at[1, k]),
            )
        )
        start_or_wait(copies[-1], whole, "start")
    for copy in copies:
        start_or_wait(copy, whole, "wait")
    if own:
        factor_copy.wait()


def start_or_wait(copy, whole, action):
    inside, *both = copy

    def run():
        for one in both:
            getattr(one, action)()

    if whole:
        run()
    else:
        pl.when(inside)(run)


def new_feedback(own, stacked, pieces, combined, columns, last):
    rows = combined.shape[0]
    given = pieces if own else [pieces]
    chips = len(pieces) if own else pieces.shape[0]
    rank, width = given[0].shape[-2:]
    outs = 3 if own else 2

    def kernel(stacked, *refs):
        parts, rest = refs[: len(given)], refs[len(given) :]
        if own:
            combined, factor, feedback, right, factor_out, *scratch = rest
        else:
            parts = [parts[0].at[k] for k in range(chips)]
            combined, _, _, feedback, right, *scratch = rest
            factor = factor_out = None
        feedback_kernel(own, columns, stacked, parts, combined, factor, feedback, right, factor_out, *scratch)

    return pl.pallas_call(
        kernel,
        in_specs=[VMEM] * (2 + len(given)) + ([VMEM] if own else [ANY] * 2),
        out_specs=[ANY] * outs,
        out_shape=[
            pltpu.HBM((rows, columns), F32),
            pltpu.HBM((rank, columns), F32),
            pltpu.HBM((rank, rows), F32),
        ][:outs],
        input_output_aliases={} if own else {3: 0, 4: 1},
        scratch_shapes=[
            pltpu.VMEM((chips, rows, width), F32),
            pltpu.SemaphoreType.DMA((2, chips)),
            pltpu.SemaphoreType.DMA,
        ],
        compiler_params=params(16),
        cost_estimate=cost(8 * rows * chips * width * rank, 4 * rows * chips * width),
        name="feedback",
    )(stacked, *given, combined, *last)


def swap(x, axis, mask):
    size = lax.axis_size(axis)
    return lax.ppermute(x, axis, [(i, i ^ mask) for i in range(size)])


def tree(terms):
    while len(terms) > 1:
        terms = [a + b for a, b in zip(terms[::2], terms[1::2])]
    return terms[0]


def sum_over(x, axis, low, high):
    while low < high:
        step = min(2, high - low)
        x = tree([x] + [swap(x, axis, k << low) for k in range(1, 1 << step)])
        low += step
    return x


def bits(axis):
    size = lax.axis_size(axis)
    assert size & (size - 1) == 0
    return size.bit_length() - 1


def per_device(gradient, feedback, right_factor):
    gradient, feedback = gradient[0], feedback[0]
    columns = gradient.shape[1]
    replicas = lax.axis_size("dp")
    chips = replicas // 2
    width = -(-columns // (replicas * 128)) * 128
    assert columns % width == 0

    given = [keep(x, pltpu.HBM) for x in (gradient, feedback, right_factor.T)]
    combined, high, low, left = left_product(*given, replicas * width)
    combined, high, low = (keep(x, pltpu.VMEM) for x in (combined, high, low))
    left = sum_over(left, "dp", 1, bits("dp"))
    left = sum_over(left, "tensor", 0, bits("tensor"))

    beside = swap(left, "dp", 1)
    theirs, half = (right_product(side, left, high, low, chips, width) for side in (False, True))
    theirs = swap(right_product(False, beside, high, low, chips, width, theirs), "dp", 1)
    half = right_product(True, beside, high, low, chips, width, half)
    left = (left + beside) / replicas
    own, *away = share(half, theirs)
    own = tree([own] + [swap(x, "dp", 2 * k) for k, x in enumerate(away, 1)])

    inverse, factor, stacked = factors(left)
    own = jnp.dot(inverse, own, precision=HIGHEST, preferred_element_type=F32) / replicas**2

    got = [own] + [swap(own, "dp", 2 * k) for k in range(1, chips)]
    other = swap(jnp.stack(got), "dp", 1)
    *outs, factor = new_feedback(True, stacked, got, combined, columns, [factor])
    outs = new_feedback(False, stacked, other, combined, columns, outs)
    return (outs[0][None], factor.T, outs[1].T)


def solution(mesh):
    return jax.shard_map(
        per_device,
        mesh=mesh,
        in_specs=(P("dp", None, "tensor"), P("dp", None, "tensor"), P("tensor", None)),
        out_specs=(P("dp", None, "tensor"), P(), P("tensor", None)),
        check_vma=False,
    )
```

```python
import functools

import jax
import jax.numpy as jnp
from jax import lax
from jax.experimental import pallas as pl
from jax.experimental.pallas import tpu as pltpu
from jax.sharding import PartitionSpec as P

F32, BF16 = jnp.float32, jnp.bfloat16
HIGHEST = lax.Precision.HIGHEST
ANY = pl.BlockSpec(memory_space=pl.ANY)
VMEM = pl.BlockSpec(memory_space=pltpu.VMEM)


def split(x):
    high = x.astype(BF16)
    return high, (x - high.astype(F32)).astype(BF16)


def dot(a, b, a_dim, b_dim, precision=None):
    return lax.dot_general(a, b, (((a_dim,), (b_dim,)), ((), ())), precision=precision, preferred_element_type=F32)


def keep(x, space):
    return pltpu.with_memory_space_constraint(x, space)


def position():
    me = lax.axis_index("dp")
    return lax.rem(me, 2), lax.div(me, 2)


def params(mebibytes):
    return pltpu.CompilerParams(vmem_limit_bytes=mebibytes << 20)


def cost(flops, bytes_accessed):
    return pl.CostEstimate(flops=int(flops), bytes_accessed=int(bytes_accessed), transcendentals=0)


def left_kernel(chunk, gradient, feedback, right, combined, high, low, left, gradient_buf, right_buf, sems):
    rows, columns = gradient.shape
    rank = right.shape[0]
    blocks = [pl.ds(i * chunk, chunk) for i in range(columns // chunk)]
    copies = []
    for i, at in enumerate(blocks):
        group = [
            pltpu.make_async_copy(gradient.at[:, at], gradient_buf.at[:, at], sems.at[0, i]),
            pltpu.make_async_copy(feedback.at[:, at], combined.at[:, at], sems.at[1, i]),
            pltpu.make_async_copy(right.at[:, at], right_buf.at[:, at], sems.at[2, i]),
        ]
        for copy in group:
            copy.start()
        copies.append(group)
    padded = combined.shape[1]
    if padded > columns:
        rest = pl.ds(columns, padded - columns)
        combined[:, rest] = jnp.zeros((rows, padded - columns), F32)
        high[:, rest] = jnp.zeros((rows, padded - columns), BF16)
        low[:, rest] = jnp.zeros((rows, padded - columns), BF16)
    total = jnp.zeros((rows, 2 * rank), F32)
    for at, group in zip(blocks, copies):
        for copy in group:
            copy.wait()
        both = jnp.concatenate(split(right_buf[:, at]), axis=0)
        c = combined[:, at] + gradient_buf[:, at].astype(F32)
        c_high, c_low = split(c)
        combined[:, at] = c
        high[:, at] = c_high
        low[:, at] = c_low
        total += dot(c_high, both, 1, 1) + dot(c_low, both, 1, 1)
    left[...] = (total[:, :rank] + total[:, rank:]).T


def left_product(gradient, feedback, right, padded):
    rows, columns = gradient.shape
    rank = right.shape[0]
    chunk = next(c for c in (1024, 512, 128) if columns % c == 0)
    return pl.pallas_call(
        functools.partial(left_kernel, chunk),
        in_specs=[ANY] * 3,
        out_specs=[VMEM] * 4,
        out_shape=[
            pltpu.VMEM((rows, padded), F32),
            pltpu.VMEM((rows, padded), BF16),
            pltpu.VMEM((rows, padded), BF16),
            pltpu.VMEM((rank, rows), F32),
        ],
        scratch_shapes=[
            pltpu.VMEM((rows, columns), BF16),
            pltpu.VMEM((rank, columns), F32),
            pltpu.SemaphoreType.DMA((3, columns // chunk)),
        ],
        compiler_params=params(16),
        cost_estimate=cost(8 * rows * columns * rank, 6 * rows * columns),
        name="left",
    )(gradient, feedback, right)


def right_kernel(own, left, high, low, pieces):
    chips, rank, width = pieces.shape
    half = chips * width
    core, _ = position()
    side = core if own else 1 - core
    block = 512 if half % 512 == 0 else 128
    both = jnp.concatenate(split(left[...]), axis=0)
    for i in range(half // block):
        at = pl.ds(pl.multiple_of(side * half + i * block, block), block)
        total = dot(both, high[:, at], 1, 0) + dot(both, low[:, at], 1, 0)
        total = total[:rank] + total[rank:]
        start = i * block
        while start < (i + 1) * block:
            piece = start // width
            stop = min((i + 1) * block, (piece + 1) * width)
            pieces[piece, :, start - piece * width : stop - piece * width] = total[:, start - i * block : stop - i * block]
            start = stop


def right_product(own, left, high, low, chips, width):
    rank, rows = left.shape
    return pl.pallas_call(
        functools.partial(right_kernel, own),
        in_specs=[VMEM] * 3,
        out_specs=VMEM,
        out_shape=pltpu.VMEM((chips, rank, width), F32),
        compiler_params=params(8),
        cost_estimate=cost(8 * rows * chips * width * rank, 4 * rows * chips * width),
        name="right",
    )(left, high, low)


def share_kernel(a, b, *outs):
    _, chip = position()
    for k, out in enumerate(outs):
        out[...] = a[chip ^ k] + b[chip ^ k]


def share(a, b):
    chips, rank, width = a.shape
    return pl.pallas_call(
        share_kernel,
        in_specs=[VMEM] * 2,
        out_specs=[VMEM] * chips,
        out_shape=[pltpu.VMEM((rank, width), F32)] * chips,
        compiler_params=params(8),
        cost_estimate=cost(chips * rank * width, 12 * chips * rank * width),
        name="share",
    )(a, b)


def factor_kernel(left, inverse, factor, stacked):
    rank, rows = left.shape
    values = left[...]
    gram = dot(values, values, 1, 1, HIGHEST)
    row = lax.broadcasted_iota(jnp.int32, (rank, rank), 0)
    column = lax.broadcasted_iota(jnp.int32, (rank, rank), 1)
    unit = (row == column).astype(F32)
    wide = jnp.concatenate([gram, unit], axis=1)
    row_of = lax.broadcasted_iota(jnp.int32, (rank, 1), 0)
    for j in range(rank - 1):
        pivot = wide[j : j + 1, :]
        scaled = pivot * (1.0 / pivot[:, j : j + 1])
        wide = wide - jnp.where(row_of > j, wide[:, j : j + 1], 0.0) * scaled
    diagonal = jnp.sum(wide[:, :rank] * unit, axis=1, keepdims=True)
    inv = wide[:, rank:] * (1.0 / jnp.sqrt(diagonal))
    inverse[...] = inv
    q = dot(inv, values, 1, 0, HIGHEST)
    factor[...] = q
    q_high, q_low = (part.astype(F32) for part in split(q))
    stacked[...] = jnp.concatenate([q_high, q_low, q_high, q_low], axis=0).T.astype(BF16)


def factors(left):
    rank, rows = left.shape
    return pl.pallas_call(
        factor_kernel,
        in_specs=[VMEM],
        out_specs=[VMEM] * 3,
        out_shape=[
            pltpu.VMEM((rank, rank), F32),
            pltpu.VMEM((rank, rows), F32),
            pltpu.VMEM((rows, 4 * rank), BF16),
        ],
        compiler_params=params(8),
        cost_estimate=cost(2e9, 1e6),
        name="factor",
    )(left)


def feedback_kernel(own, columns, stacked, pieces, combined, factor, feedback, right, factor_out, feedback_buf, sems, factor_sem):
    rank = pieces[0].shape[-2]
    chips, rows, width = feedback_buf.shape
    whole = combined.shape[1] == columns
    core, chip = position()
    side = core if own else 1 - core
    copies = []
    if own:
        factor_copy = pltpu.make_async_copy(factor, factor_out, factor_sem)
        factor_copy.start()
    for k in range(chips):
        place = side * chips + (chip ^ k)
        at = pl.ds(pl.multiple_of(place * width, 128), width)
        piece = pieces[k]
        piece_high, piece_low = split(piece[...])
        four = jnp.concatenate([piece_high, piece_high, piece_low, piece_low], axis=0)
        feedback_buf[k] = combined[:, at] - dot(stacked[...], four, 1, 0)
        copies.append(
            (
                place * width < columns,
                pltpu.make_async_copy(feedback_buf.at[k], feedback.at[:, at], sems.at[0, k]),
                pltpu.make_async_copy(piece, right.at[:, at], sems.at[1, k]),
            )
        )
        start_or_wait(copies[-1], whole, "start")
    for copy in copies:
        start_or_wait(copy, whole, "wait")
    if own:
        factor_copy.wait()


def start_or_wait(copy, whole, action):
    inside, *both = copy

    def run():
        for one in both:
            getattr(one, action)()

    if whole:
        run()
    else:
        pl.when(inside)(run)


def new_feedback(own, stacked, pieces, combined, columns, last):
    rows = combined.shape[0]
    given = pieces if own else [pieces]
    chips = len(pieces) if own else pieces.shape[0]
    rank, width = given[0].shape[-2:]
    outs = 3 if own else 2

    def kernel(stacked, *refs):
        parts, rest = refs[: len(given)], refs[len(given) :]
        if own:
            combined, factor, feedback, right, factor_out, *scratch = rest
        else:
            parts = [parts[0].at[k] for k in range(chips)]
            combined, _, _, feedback, right, *scratch = rest
            factor = factor_out = None
        feedback_kernel(own, columns, stacked, parts, combined, factor, feedback, right, factor_out, *scratch)

    return pl.pallas_call(
        kernel,
        in_specs=[VMEM] * (2 + len(given)) + ([VMEM] if own else [ANY] * 2),
        out_specs=[ANY] * outs,
        out_shape=[
            pltpu.HBM((rows, columns), F32),
            pltpu.HBM((rank, columns), F32),
            pltpu.HBM((rank, rows), F32),
        ][:outs],
        input_output_aliases={} if own else {3: 0, 4: 1},
        scratch_shapes=[
            pltpu.VMEM((chips, rows, width), F32),
            pltpu.SemaphoreType.DMA((2, chips)),
            pltpu.SemaphoreType.DMA,
        ],
        compiler_params=params(16),
        cost_estimate=cost(8 * rows * chips * width * rank, 4 * rows * chips * width),
        name="feedback",
    )(stacked, *given, combined, *last)


def swap(x, axis, mask):
    size = lax.axis_size(axis)
    return lax.ppermute(x, axis, [(i, i ^ mask) for i in range(size)])


def tree(terms):
    while len(terms) > 1:
        terms = [a + b for a, b in zip(terms[::2], terms[1::2])]
    return terms[0]


def lead(dim, mask):
    pairs = []
    for i in range(1, lax.axis_size("dp"), 2):
        for j in range(lax.axis_size("tensor")):
            there = (i ^ mask, j) if dim == 0 else (i, j ^ mask)
            pairs.append((index_of(i, j), index_of(*there)))
    return pairs


def index_of(i, j):
    return i * lax.axis_size("tensor") + j


def sum_over(x, dim, low, high):
    while low < high:
        step = min(2, high - low)
        came = [lax.ppermute(x, ("dp", "tensor"), lead(dim, k << low)) for k in range(1, 1 << step)]
        x = tree([x] + came)
        low += step
    return x


def hand_over(x):
    pairs = [(i, i - 1) for i in range(1, lax.axis_size("dp"), 2)]
    return lax.ppermute(x, "dp", pairs)


def settle_kernel(mine, came, out):
    core, _ = position()
    out[...] = jnp.where(core == 1, mine[...], came[...])


def settle(mine, came):
    return pl.pallas_call(
        settle_kernel,
        in_specs=[VMEM] * 2,
        out_specs=VMEM,
        out_shape=pltpu.VMEM(mine.shape, F32),
        compiler_params=params(8),
        cost_estimate=cost(mine.size, 12 * mine.size),
        name="settle",
    )(mine, came)


def bits(axis):
    size = lax.axis_size(axis)
    assert size & (size - 1) == 0
    return size.bit_length() - 1


def per_device(gradient, feedback, right_factor):
    gradient, feedback = gradient[0], feedback[0]
    columns = gradient.shape[1]
    replicas = lax.axis_size("dp")
    chips = replicas // 2
    width = -(-columns // (replicas * 128)) * 128
    assert columns % width == 0

    given = [keep(x, pltpu.HBM) for x in (gradient, feedback, right_factor.T)]
    combined, high, low, left = left_product(*given, replicas * width)
    combined, high, low = (keep(x, pltpu.VMEM) for x in (combined, high, low))
    left = left + swap(left, "dp", 1)
    left = sum_over(left, 0, 1, bits("dp"))
    left = sum_over(left, 1, 0, bits("tensor"))
    left = settle(left, hand_over(left)) / replicas

    theirs = swap(right_product(False, left, high, low, chips, width), "dp", 1)
    half = right_product(True, left, high, low, chips, width)
    own, *away = share(half, theirs)
    came = [swap(x, "dp", 2 * k) for k, x in enumerate(away, 1)]
    own = tree(came[::-1] + [own])

    inverse, factor, stacked = factors(left)
    own = jnp.dot(inverse, own, precision=HIGHEST, preferred_element_type=F32) / replicas

    got = [own] + [swap(own, "dp", 2 * k) for k in range(1, chips)]
    other = swap(jnp.stack(got), "dp", 1)
    *outs, factor = new_feedback(True, stacked, got, combined, columns, [factor])
    outs = new_feedback(False, stacked, other, combined, columns, outs)
    return (outs[0][None], factor.T, outs[1].T)


def solution(mesh):
    return jax.shard_map(
        per_device,
        mesh=mesh,
        in_specs=(P("dp", None, "tensor"), P("dp", None, "tensor"), P("tensor", None)),
        out_specs=(P("dp", None, "tensor"), P(), P("tensor", None)),
        check_vma=False,
    )
```

```python
import functools

import jax
import jax.numpy as jnp
from jax import lax
from jax.experimental import pallas as pl
from jax.experimental.pallas import tpu as pltpu
from jax.sharding import PartitionSpec as P

F32, BF16 = jnp.float32, jnp.bfloat16
HIGHEST = lax.Precision.HIGHEST
ANY = pl.BlockSpec(memory_space=pl.ANY)
VMEM = pl.BlockSpec(memory_space=pltpu.VMEM)


def split(x):
    high = x.astype(BF16)
    return high, (x - high.astype(F32)).astype(BF16)


def dot(a, b, a_dim, b_dim, precision=None):
    return lax.dot_general(a, b, (((a_dim,), (b_dim,)), ((), ())), precision=precision, preferred_element_type=F32)


def keep(x, space):
    return pltpu.with_memory_space_constraint(x, space)


def position():
    me = lax.axis_index("dp")
    return lax.rem(me, 2), lax.div(me, 2)


def params(mebibytes):
    return pltpu.CompilerParams(vmem_limit_bytes=mebibytes << 20)


def cost(flops, bytes_accessed):
    return pl.CostEstimate(flops=int(flops), bytes_accessed=int(bytes_accessed), transcendentals=0)


def left_kernel(chunk, gradient, feedback, right, combined, high, low, left, gradient_buf, right_buf, sems):
    rows, columns = gradient.shape
    rank = right.shape[0]
    blocks = [pl.ds(i * chunk, chunk) for i in range(columns // chunk)]
    copies = []
    for i, at in enumerate(blocks):
        group = [
            pltpu.make_async_copy(gradient.at[:, at], gradient_buf.at[:, at], sems.at[0, i]),
            pltpu.make_async_copy(feedback.at[:, at], combined.at[:, at], sems.at[1, i]),
            pltpu.make_async_copy(right.at[:, at], right_buf.at[:, at], sems.at[2, i]),
        ]
        for copy in group:
            copy.start()
        copies.append(group)
    padded = combined.shape[1]
    if padded > columns:
        rest = pl.ds(columns, padded - columns)
        combined[:, rest] = jnp.zeros((rows, padded - columns), F32)
        high[:, rest] = jnp.zeros((rows, padded - columns), BF16)
        low[:, rest] = jnp.zeros((rows, padded - columns), BF16)
    total = jnp.zeros((rows, 2 * rank), F32)
    for at, group in zip(blocks, copies):
        for copy in group:
            copy.wait()
        both = jnp.concatenate(split(right_buf[:, at]), axis=0)
        c = combined[:, at] + gradient_buf[:, at].astype(F32)
        c_high, c_low = split(c)
        combined[:, at] = c
        high[:, at] = c_high
        low[:, at] = c_low
        total += dot(c_high, both, 1, 1) + dot(c_low, both, 1, 1)
    left[...] = (total[:, :rank] + total[:, rank:]).T


def left_product(gradient, feedback, right, padded):
    rows, columns = gradient.shape
    rank = right.shape[0]
    chunk = next(c for c in (1024, 512, 128) if columns % c == 0)
    return pl.pallas_call(
        functools.partial(left_kernel, chunk),
        in_specs=[ANY] * 3,
        out_specs=[VMEM] * 4,
        out_shape=[
            pltpu.VMEM((rows, padded), F32),
            pltpu.VMEM((rows, padded), BF16),
            pltpu.VMEM((rows, padded), BF16),
            pltpu.VMEM((rank, rows), F32),
        ],
        scratch_shapes=[
            pltpu.VMEM((rows, columns), BF16),
            pltpu.VMEM((rank, columns), F32),
            pltpu.SemaphoreType.DMA((3, columns // chunk)),
        ],
        compiler_params=params(16),
        cost_estimate=cost(8 * rows * columns * rank, 6 * rows * columns),
        name="left",
    )(gradient, feedback, right)


def right_kernel(own, left, high, low, *refs):
    *before, pieces = refs
    chips, rank, width = pieces.shape
    half = chips * width
    core, _ = position()
    side = core if own else 1 - core
    block = 512 if half % 512 == 0 else 128
    both = jnp.concatenate(split(left[...]), axis=0)
    for i in range(half // block):
        at = pl.ds(pl.multiple_of(side * half + i * block, block), block)
        total = dot(both, high[:, at], 1, 0) + dot(both, low[:, at], 1, 0)
        total = total[:rank] + total[rank:]
        start = i * block
        while start < (i + 1) * block:
            piece = start // width
            stop = min((i + 1) * block, (piece + 1) * width)
            there = (piece, slice(None), slice(start - piece * width, stop - piece * width))
            part = total[:, start - i * block : stop - i * block]
            pieces[there] = before[0][there] + part if before else part
            start = stop


def right_product(own, left, high, low, chips, width, *before):
    rank, rows = left.shape
    return pl.pallas_call(
        functools.partial(right_kernel, own),
        in_specs=[VMEM] * (3 + len(before)),
        out_specs=VMEM,
        out_shape=pltpu.VMEM((chips, rank, width), F32),
        compiler_params=params(8),
        cost_estimate=cost(8 * rows * chips * width * rank, 4 * rows * chips * width),
        name="right",
    )(left, high, low, *before)


def share_kernel(a, b, *outs):
    _, chip = position()
    for k, out in enumerate(outs):
        out[...] = a[chip ^ k] + b[chip ^ k]


def share(a, b):
    chips, rank, width = a.shape
    return pl.pallas_call(
        share_kernel,
        in_specs=[VMEM] * 2,
        out_specs=[VMEM] * chips,
        out_shape=[pltpu.VMEM((rank, width), F32)] * chips,
        compiler_params=params(8),
        cost_estimate=cost(chips * rank * width, 12 * chips * rank * width),
        name="share",
    )(a, b)


def factor_kernel(left, inverse, factor, stacked):
    rank, rows = left.shape
    values = left[...]
    gram = dot(values, values, 1, 1, HIGHEST)
    row = lax.broadcasted_iota(jnp.int32, (rank, rank), 0)
    column = lax.broadcasted_iota(jnp.int32, (rank, rank), 1)
    unit = (row == column).astype(F32)
    wide = jnp.concatenate([gram, unit], axis=1)
    row_of = lax.broadcasted_iota(jnp.int32, (rank, 1), 0)
    for j in range(rank - 1):
        pivot = wide[j : j + 1, :]
        scaled = pivot * (1.0 / pivot[:, j : j + 1])
        wide = wide - jnp.where(row_of > j, wide[:, j : j + 1], 0.0) * scaled
    diagonal = jnp.sum(wide[:, :rank] * unit, axis=1, keepdims=True)
    inv = wide[:, rank:] * (1.0 / jnp.sqrt(diagonal))
    inverse[...] = inv
    q = dot(inv, values, 1, 0, HIGHEST)
    factor[...] = q
    q_high, q_low = (part.astype(F32) for part in split(q))
    stacked[...] = jnp.concatenate([q_high, q_low, q_high, q_low], axis=0).T.astype(BF16)


def factors(left):
    rank, rows = left.shape
    return pl.pallas_call(
        factor_kernel,
        in_specs=[VMEM],
        out_specs=[VMEM] * 3,
        out_shape=[
            pltpu.VMEM((rank, rank), F32),
            pltpu.VMEM((rank, rows), F32),
            pltpu.VMEM((rows, 4 * rank), BF16),
        ],
        compiler_params=params(8),
        cost_estimate=cost(2e9, 1e6),
        name="factor",
    )(left)


def feedback_kernel(own, columns, stacked, pieces, combined, factor, feedback, right, factor_out, feedback_buf, sems, factor_sem):
    rank = pieces[0].shape[-2]
    chips, rows, width = feedback_buf.shape
    whole = combined.shape[1] == columns
    core, chip = position()
    side = core if own else 1 - core
    copies = []
    if own:
        factor_copy = pltpu.make_async_copy(factor, factor_out, factor_sem)
        factor_copy.start()
    for k in range(chips):
        place = side * chips + (chip ^ k)
        at = pl.ds(pl.multiple_of(place * width, 128), width)
        piece = pieces[k]
        piece_high, piece_low = split(piece[...])
        four = jnp.concatenate([piece_high, piece_high, piece_low, piece_low], axis=0)
        feedback_buf[k] = combined[:, at] - dot(stacked[...], four, 1, 0)
        copies.append(
            (
                place * width < columns,
                pltpu.make_async_copy(feedback_buf.at[k], feedback.at[:, at], sems.at[0, k]),
                pltpu.make_async_copy(piece, right.at[:, at], sems.at[1, k]),
            )
        )
        start_or_wait(copies[-1], whole, "start")
    for copy in copies:
        start_or_wait(copy, whole, "wait")
    if own:
        factor_copy.wait()


def start_or_wait(copy, whole, action):
    inside, *both = copy

    def run():
        for one in both:
            getattr(one, action)()

    if whole:
        run()
    else:
        pl.when(inside)(run)


def new_feedback(own, stacked, pieces, combined, columns, last):
    rows = combined.shape[0]
    given = pieces if own else [pieces]
    chips = len(pieces) if own else pieces.shape[0]
    rank, width = given[0].shape[-2:]
    outs = 3 if own else 2

    def kernel(stacked, *refs):
        parts, rest = refs[: len(given)], refs[len(given) :]
        if own:
            combined, factor, feedback, right, factor_out, *scratch = rest
        else:
            parts = [parts[0].at[k] for k in range(chips)]
            combined, _, _, feedback, right, *scratch = rest
            factor = factor_out = None
        feedback_kernel(own, columns, stacked, parts, combined, factor, feedback, right, factor_out, *scratch)

    return pl.pallas_call(
        kernel,
        in_specs=[VMEM] * (2 + len(given)) + ([VMEM] if own else [ANY] * 2),
        out_specs=[ANY] * outs,
        out_shape=[
            pltpu.HBM((rows, columns), F32),
            pltpu.HBM((rank, columns), F32),
            pltpu.HBM((rank, rows), F32),
        ][:outs],
        input_output_aliases={} if own else {3: 0, 4: 1},
        scratch_shapes=[
            pltpu.VMEM((chips, rows, width), F32),
            pltpu.SemaphoreType.DMA((2, chips)),
            pltpu.SemaphoreType.DMA,
        ],
        compiler_params=params(16),
        cost_estimate=cost(8 * rows * chips * width * rank, 4 * rows * chips * width),
        name="feedback",
    )(stacked, *given, combined, *last)


def swap(x, axis, mask):
    size = lax.axis_size(axis)
    return lax.ppermute(x, axis, [(i, i ^ mask) for i in range(size)])


def tree(terms):
    while len(terms) > 1:
        terms = [a + b for a, b in zip(terms[::2], terms[1::2])]
    return terms[0]


def steps(low, high):
    return [(i, min(2, high - i)) for i in range(low, high, 2)]


def sum_stage(x, axis, low, count):
    if count == 1:
        return x + swap(x, axis, 1 << low)
    first = lax.ppermute(x, ("dp", "tensor"), pairs_of(axis, 1 << low, 3 << low))
    second = lax.ppermute(x, ("dp", "tensor"), pairs_of(axis, 1 << low, 2 << low))
    return part(x, first, second)


def pairs_of(axis, *masks):
    pairs = []
    for i in range(lax.axis_size("dp")):
        for j in range(lax.axis_size("tensor")):
            mask = masks[i % 2]
            there = (i ^ mask, j) if axis == "dp" else (i, j ^ mask)
            pairs.append(tuple(a * lax.axis_size("tensor") + b for a, b in ((i, j), there)))
    return pairs


def part_kernel(mine, first, second, out):
    core, _ = position()
    out[...] = first[...] + jnp.where(core == 1, second[...], mine[...])


def part(mine, first, second):
    return pl.pallas_call(
        part_kernel,
        in_specs=[VMEM] * 3,
        out_specs=VMEM,
        out_shape=pltpu.VMEM(mine.shape, F32),
        compiler_params=params(8),
        cost_estimate=cost(mine.size, 16 * mine.size),
        name="part",
    )(mine, first, second)


def bits(axis):
    size = lax.axis_size(axis)
    assert size & (size - 1) == 0
    return size.bit_length() - 1


def per_device(gradient, feedback, right_factor):
    gradient, feedback = gradient[0], feedback[0]
    columns = gradient.shape[1]
    replicas = lax.axis_size("dp")
    chips = replicas // 2
    width = -(-columns // (replicas * 128)) * 128
    assert columns % width == 0

    given = [keep(x, pltpu.HBM) for x in (gradient, feedback, right_factor.T)]
    combined, high, low, left = left_product(*given, replicas * width)
    combined, high, low = (keep(x, pltpu.VMEM) for x in (combined, high, low))
    left = left + swap(left, "dp", 1)
    stages = [("dp", low, count) for low, count in steps(1, bits("dp"))]
    stages += [("tensor", low, count) for low, count in steps(0, bits("tensor"))]
    stages.sort(key=lambda stage: stage[2])
    for i, stage in enumerate(stages):
        left = sum_stage(left, *stage)
        if stage[2] == 2 and i < len(stages) - 1:
            left = left + swap(left, "dp", 1)
    if stages[-1][2] == 1:
        left = left * 0.5
    beside = swap(left, "dp", 1)
    theirs, half = (right_product(side, left, high, low, chips, width) for side in (False, True))
    theirs = swap(right_product(False, beside, high, low, chips, width, theirs), "dp", 1)
    half = right_product(True, beside, high, low, chips, width, half)
    left = (left + beside) / replicas
    own, *away = share(half, theirs)
    own = tree([own] + [swap(x, "dp", 2 * k) for k, x in enumerate(away, 1)])

    inverse, factor, stacked = factors(left)
    own = jnp.dot(inverse, own, precision=HIGHEST, preferred_element_type=F32) / replicas**2

    got = [own] + [swap(own, "dp", 2 * k) for k in range(1, chips)]
    other = swap(jnp.stack(got), "dp", 1)
    *outs, factor = new_feedback(True, stacked, got, combined, columns, [factor])
    outs = new_feedback(False, stacked, other, combined, columns, outs)
    return (outs[0][None], factor.T, outs[1].T)


def solution(mesh):
    return jax.shard_map(
        per_device,
        mesh=mesh,
        in_specs=(P("dp", None, "tensor"), P("dp", None, "tensor"), P("tensor", None)),
        out_specs=(P("dp", None, "tensor"), P(), P("tensor", None)),
        check_vma=False,
    )
```

```python
import functools

import jax
import jax.numpy as jnp
from jax import lax
from jax.experimental import pallas as pl
from jax.experimental.pallas import tpu as pltpu
from jax.sharding import PartitionSpec as P

F32, BF16 = jnp.float32, jnp.bfloat16
HIGHEST = lax.Precision.HIGHEST
ANY = pl.BlockSpec(memory_space=pl.ANY)
VMEM = pl.BlockSpec(memory_space=pltpu.VMEM)


def split(x):
    high = x.astype(BF16)
    return high, (x - high.astype(F32)).astype(BF16)


def dot(a, b, a_dim, b_dim, precision=None):
    return lax.dot_general(a, b, (((a_dim,), (b_dim,)), ((), ())), precision=precision, preferred_element_type=F32)


def keep(x, space):
    return pltpu.with_memory_space_constraint(x, space)


def position():
    me = lax.axis_index("dp")
    return lax.rem(me, 2), lax.div(me, 2)


def params(mebibytes):
    return pltpu.CompilerParams(vmem_limit_bytes=mebibytes << 20)


def cost(flops, bytes_accessed):
    return pl.CostEstimate(flops=int(flops), bytes_accessed=int(bytes_accessed), transcendentals=0)


def left_kernel(chunk, gradient, feedback, right, combined, high, low, left, gradient_buf, right_buf, sems):
    rows, columns = gradient.shape
    rank = right.shape[0]
    blocks = [pl.ds(i * chunk, chunk) for i in range(columns // chunk)]
    copies = []
    for i, at in enumerate(blocks):
        group = [
            pltpu.make_async_copy(gradient.at[:, at], gradient_buf.at[:, at], sems.at[0, i]),
            pltpu.make_async_copy(feedback.at[:, at], combined.at[:, at], sems.at[1, i]),
            pltpu.make_async_copy(right.at[:, at], right_buf.at[:, at], sems.at[2, i]),
        ]
        for copy in group:
            copy.start()
        copies.append(group)
    padded = combined.shape[1]
    if padded > columns:
        rest = pl.ds(columns, padded - columns)
        combined[:, rest] = jnp.zeros((rows, padded - columns), F32)
        high[:, rest] = jnp.zeros((rows, padded - columns), BF16)
        low[:, rest] = jnp.zeros((rows, padded - columns), BF16)
    total = jnp.zeros((rows, 2 * rank), F32)
    for at, group in zip(blocks, copies):
        for copy in group:
            copy.wait()
        both = jnp.concatenate(split(right_buf[:, at]), axis=0)
        c = combined[:, at] + gradient_buf[:, at].astype(F32)
        c_high, c_low = split(c)
        combined[:, at] = c
        high[:, at] = c_high
        low[:, at] = c_low
        total += dot(c_high, both, 1, 1) + dot(c_low, both, 1, 1)
    left[...] = (total[:, :rank] + total[:, rank:]).T


def left_product(gradient, feedback, right, padded):
    rows, columns = gradient.shape
    rank = right.shape[0]
    chunk = next(c for c in (1024, 512, 128) if columns % c == 0)
    return pl.pallas_call(
        functools.partial(left_kernel, chunk),
        in_specs=[ANY] * 3,
        out_specs=[VMEM] * 4,
        out_shape=[
            pltpu.VMEM((rows, padded), F32),
            pltpu.VMEM((rows, padded), BF16),
            pltpu.VMEM((rows, padded), BF16),
            pltpu.VMEM((rank, rows), F32),
        ],
        scratch_shapes=[
            pltpu.VMEM((rows, columns), BF16),
            pltpu.VMEM((rank, columns), F32),
            pltpu.SemaphoreType.DMA((3, columns // chunk)),
        ],
        compiler_params=params(16),
        cost_estimate=cost(8 * rows * columns * rank, 6 * rows * columns),
        name="left",
    )(gradient, feedback, right)


def right_kernel(own, left, high, low, *refs):
    *before, pieces = refs
    chips, rank, width = pieces.shape
    half = chips * width
    core, _ = position()
    side = core if own else 1 - core
    block = 512 if half % 512 == 0 else 128
    both = jnp.concatenate(split(left[...]), axis=0)
    for i in range(half // block):
        at = pl.ds(pl.multiple_of(side * half + i * block, block), block)
        total = dot(both, high[:, at], 1, 0) + dot(both, low[:, at], 1, 0)
        total = total[:rank] + total[rank:]
        start = i * block
        while start < (i + 1) * block:
            piece = start // width
            stop = min((i + 1) * block, (piece + 1) * width)
            there = (piece, slice(None), slice(start - piece * width, stop - piece * width))
            part = total[:, start - i * block : stop - i * block]
            pieces[there] = before[0][there] + part if before else part
            start = stop


def right_product(own, left, high, low, chips, width, *before):
    rank, rows = left.shape
    return pl.pallas_call(
        functools.partial(right_kernel, own),
        in_specs=[VMEM] * (3 + len(before)),
        out_specs=VMEM,
        out_shape=pltpu.VMEM((chips, rank, width), F32),
        compiler_params=params(8),
        cost_estimate=cost(8 * rows * chips * width * rank, 4 * rows * chips * width),
        name="right",
    )(left, high, low, *before)


def factor_kernel(scale, left, inverse, factor, stacked):
    rank, rows = left.shape
    values = left[...]
    gram = dot(values, values, 1, 1, HIGHEST)
    row = lax.broadcasted_iota(jnp.int32, (rank, rank), 0)
    column = lax.broadcasted_iota(jnp.int32, (rank, rank), 1)
    unit = (row == column).astype(F32)
    wide = jnp.concatenate([gram, unit], axis=1)
    row_of = lax.broadcasted_iota(jnp.int32, (rank, 1), 0)
    for j in range(rank - 1):
        pivot = wide[j : j + 1, :]
        scaled = pivot * (1.0 / pivot[:, j : j + 1])
        wide = wide - jnp.where(row_of > j, wide[:, j : j + 1], 0.0) * scaled
    diagonal = jnp.sum(wide[:, :rank] * unit, axis=1, keepdims=True)
    inv = wide[:, rank:] * (1.0 / jnp.sqrt(diagonal))
    inverse[...] = inv * scale
    q = dot(inv, values, 1, 0, HIGHEST)
    factor[...] = q
    q_high, q_low = (part.astype(F32) for part in split(q))
    stacked[...] = jnp.concatenate([q_high, q_low, q_high, q_low], axis=0).T.astype(BF16)


def factors(left, scale):
    rank, rows = left.shape
    return pl.pallas_call(
        functools.partial(factor_kernel, scale),
        in_specs=[VMEM],
        out_specs=[VMEM] * 3,
        out_shape=[
            pltpu.VMEM((rank, rank), F32),
            pltpu.VMEM((rank, rows), F32),
            pltpu.VMEM((rows, 4 * rank), BF16),
        ],
        compiler_params=params(8),
        cost_estimate=cost(2e9, 1e6),
        name="factor",
    )(left)


def feedback_kernel(own, columns, stacked, inverse, pieces, combined, factor, feedback, right, factor_out, feedback_buf, right_buf, sems, factor_sem):
    chips, rows, width = feedback_buf.shape
    whole = combined.shape[1] == columns
    core, _ = position()
    side = core if own else 1 - core
    copies = []
    if own:
        factor_copy = pltpu.make_async_copy(factor, factor_out, factor_sem)
        factor_copy.start()
    for k in range(chips):
        place = side * chips + k
        at = pl.ds(pl.multiple_of(place * width, 128), width)
        piece = dot(inverse[...], pieces[k][...], 1, 0, HIGHEST)
        right_buf[k] = piece
        piece_high, piece_low = split(piece)
        four = jnp.concatenate([piece_high, piece_high, piece_low, piece_low], axis=0)
        feedback_buf[k] = combined[:, at] - dot(stacked[...], four, 1, 0)
        copies.append(
            (
                place * width < columns,
                pltpu.make_async_copy(feedback_buf.at[k], feedback.at[:, at], sems.at[0, k]),
                pltpu.make_async_copy(right_buf.at[k], right.at[:, at], sems.at[1, k]),
            )
        )
        start_or_wait(copies[-1], whole, "start")
    for copy in copies:
        start_or_wait(copy, whole, "wait")
    if own:
        factor_copy.wait()


def start_or_wait(copy, whole, action):
    inside, *both = copy

    def run():
        for one in both:
            getattr(one, action)()

    if whole:
        run()
    else:
        pl.when(inside)(run)


def new_feedback(own, stacked, inverse, given, combined, columns, last):
    rows = combined.shape[0]
    chips = sum(x.shape[0] for x in given)
    rank, width = given[0].shape[-2:]
    outs = 3 if own else 2
    first = 3 + len(given)

    def kernel(stacked, inverse, *refs):
        parts = [x.at[k] for x in refs[: len(given)] for k in range(x.shape[0])]
        if own:
            combined, factor, feedback, right, factor_out, *scratch = refs[len(given) :]
        else:
            combined, _, _, feedback, right, *scratch = refs[len(given) :]
            factor = factor_out = None
        feedback_kernel(own, columns, stacked, inverse, parts, combined, factor, feedback, right, factor_out, *scratch)

    return pl.pallas_call(
        kernel,
        in_specs=[VMEM] * first + ([VMEM] if own else [ANY] * 2),
        out_specs=[ANY] * outs,
        out_shape=[
            pltpu.HBM((rows, columns), F32),
            pltpu.HBM((rank, columns), F32),
            pltpu.HBM((rank, rows), F32),
        ][:outs],
        input_output_aliases={} if own else {first: 0, first + 1: 1},
        scratch_shapes=[
            pltpu.VMEM((chips, rows, width), F32),
            pltpu.VMEM((chips, rank, width), F32),
            pltpu.SemaphoreType.DMA((2, chips)),
            pltpu.SemaphoreType.DMA,
        ],
        compiler_params=params(16),
        cost_estimate=cost(8 * rows * chips * width * rank, 4 * rows * chips * width),
        name="feedback",
    )(stacked, inverse, *given, combined, *last)


def swap(x, axis, mask):
    size = lax.axis_size(axis)
    return lax.ppermute(x, axis, [(i, i ^ mask) for i in range(size)])


def steps(low, high):
    return [(i, min(2, high - i)) for i in range(low, high, 2)]


def sum_stage(x, axis, low, count):
    if count == 1:
        return x + swap(x, axis, 1 << low)
    first = lax.ppermute(x, ("dp", "tensor"), pairs_of(axis, 1 << low, 3 << low))
    second = lax.ppermute(x, ("dp", "tensor"), pairs_of(axis, 1 << low, 2 << low))
    return part(x, first, second)


def pairs_of(axis, *masks):
    pairs = []
    for i in range(lax.axis_size("dp")):
        for j in range(lax.axis_size("tensor")):
            mask = masks[i % 2]
            there = (i ^ mask, j) if axis == "dp" else (i, j ^ mask)
            pairs.append(tuple(a * lax.axis_size("tensor") + b for a, b in ((i, j), there)))
    return pairs


def part_kernel(mine, first, second, out):
    core, _ = position()
    out[...] = first[...] + jnp.where(core == 1, second[...], mine[...])


def part(mine, first, second):
    return pl.pallas_call(
        part_kernel,
        in_specs=[VMEM] * 3,
        out_specs=VMEM,
        out_shape=pltpu.VMEM(mine.shape, F32),
        compiler_params=params(8),
        cost_estimate=cost(mine.size, 16 * mine.size),
        name="part",
    )(mine, first, second)


def after(x, token):
    return lax.optimization_barrier((x, token))[0]


def bits(axis):
    size = lax.axis_size(axis)
    assert size & (size - 1) == 0
    return size.bit_length() - 1


def per_device(gradient, feedback, right_factor):
    gradient, feedback = gradient[0], feedback[0]
    columns = gradient.shape[1]
    replicas = lax.axis_size("dp")
    chips = replicas // 2
    width = -(-columns // (replicas * 128)) * 128
    assert columns % width == 0

    given = [keep(x, pltpu.HBM) for x in (gradient, feedback, right_factor.T)]
    combined, high, low, left = left_product(*given, replicas * width)
    combined, high, low = (keep(x, pltpu.VMEM) for x in (combined, high, low))
    left = left + swap(left, "dp", 1)
    stages = [("dp", low, count) for low, count in steps(1, bits("dp"))]
    stages += [("tensor", low, count) for low, count in steps(0, bits("tensor"))]
    stages.sort(key=lambda stage: stage[2])
    for i, stage in enumerate(stages):
        left = sum_stage(left, *stage)
        if stage[2] == 2 and i < len(stages) - 1:
            left = left + swap(left, "dp", 1)
    if stages[-1][2] == 1:
        left = left * 0.5
    beside = swap(left, "dp", 1)
    theirs, half = (right_product(side, left, high, low, chips, width) for side in (False, True))
    theirs = swap(right_product(False, beside, high, low, chips, width, theirs), "dp", 1)
    half = right_product(True, beside, high, low, chips, width, half)
    left = (left + beside) / replicas
    masks = [1 << i for i in range(1, bits("dp"))]
    parts = [half[: chips // 2] + theirs[: chips // 2], half[chips // 2 :] + theirs[chips // 2 :]]
    inverse, factor, stacked = factors(left, 1.0 / replicas**2)
    for i, pair in enumerate(zip(masks, masks[::-1])):
        came = [swap(x, "dp", mask) for x, mask in zip(parts, pair)]
        if i == 0:
            came = [after(x, inverse) for x in came]
        parts = [x + y for x, y in zip(parts, came)]

    other = swap(jnp.concatenate(parts), "dp", 1)
    *outs, factor = new_feedback(True, stacked, inverse, parts, combined, columns, [factor])
    outs = new_feedback(False, stacked, inverse, [other], combined, columns, outs)
    return (outs[0][None], factor.T, outs[1].T)


def solution(mesh):
    return jax.shard_map(
        per_device,
        mesh=mesh,
        in_specs=(P("dp", None, "tensor"), P("dp", None, "tensor"), P("tensor", None)),
        out_specs=(P("dp", None, "tensor"), P(), P("tensor", None)),
        check_vma=False,
    )
```

```python
import functools

import jax
import jax.numpy as jnp
from jax import lax
from jax.experimental import pallas as pl
from jax.experimental.pallas import tpu as pltpu
from jax.sharding import PartitionSpec as P

F32, BF16 = jnp.float32, jnp.bfloat16
BLOCK = 256
HIGHEST = lax.Precision.HIGHEST
ANY = pl.BlockSpec(memory_space=pl.ANY)
VMEM = pl.BlockSpec(memory_space=pltpu.VMEM)


def split(x):
    high = x.astype(BF16)
    return high, (x - high.astype(F32)).astype(BF16)


def dot(a, b, a_dim, b_dim, precision=None):
    return lax.dot_general(a, b, (((a_dim,), (b_dim,)), ((), ())), precision=precision, preferred_element_type=F32)


def keep(x, space):
    return pltpu.with_memory_space_constraint(x, space)


def position():
    me = lax.axis_index("dp")
    return lax.rem(me, 2), lax.div(me, 2)


def params(mebibytes):
    return pltpu.CompilerParams(vmem_limit_bytes=mebibytes << 20)


def cost(flops, bytes_accessed):
    return pl.CostEstimate(flops=int(flops), bytes_accessed=int(bytes_accessed), transcendentals=0)


def left_kernel(chunk, gradient, feedback, right, high, low, left, gradient_buf, feedback_buf, right_buf, sems):
    rows, columns = gradient.shape
    rank = right.shape[0]
    blocks = [pl.ds(i * chunk, chunk) for i in range(columns // chunk)]
    copies = []
    for i, at in enumerate(blocks):
        group = [
            pltpu.make_async_copy(gradient.at[:, at], gradient_buf.at[:, at], sems.at[0, i]),
            pltpu.make_async_copy(feedback.at[:, at], feedback_buf.at[:, at], sems.at[1, i]),
            pltpu.make_async_copy(right.at[:, at], right_buf.at[:, at], sems.at[2, i]),
        ]
        for copy in group:
            copy.start()
        copies.append(group)
    padded = high.shape[1]
    if padded > columns:
        rest = pl.ds(columns, padded - columns)
        high[:, rest] = jnp.zeros((rows, padded - columns), BF16)
        low[:, rest] = jnp.zeros((rows, padded - columns), BF16)
    total = jnp.zeros((rows, 2 * rank), F32)
    for at, group in zip(blocks, copies):
        for copy in group:
            copy.wait()
        both = jnp.concatenate(split(right_buf[:, at]), axis=0)
        c_high, c_low = split(feedback_buf[:, at] + gradient_buf[:, at].astype(F32))
        high[:, at] = c_high
        low[:, at] = c_low
        total += dot(c_high, both, 1, 1) + dot(c_low, both, 1, 1)
    left[...] = (total[:, :rank] + total[:, rank:]).T


def left_product(gradient, feedback, right, padded):
    rows, columns = gradient.shape
    rank = right.shape[0]
    chunk = next(c for c in (1024, 512, 128) if columns % c == 0)
    return pl.pallas_call(
        functools.partial(left_kernel, chunk),
        in_specs=[ANY] * 3,
        out_specs=[VMEM] * 3,
        out_shape=[
            pltpu.VMEM((rows, padded), BF16),
            pltpu.VMEM((rows, padded), BF16),
            pltpu.VMEM((rank, rows), F32),
        ],
        scratch_shapes=[
            pltpu.VMEM((rows, columns), BF16),
            pltpu.VMEM((rows, columns), F32),
            pltpu.VMEM((rank, columns), F32),
            pltpu.SemaphoreType.DMA((3, columns // chunk)),
        ],
        compiler_params=params(16),
        cost_estimate=cost(8 * rows * columns * rank, 6 * rows * columns),
        name="left",
    )(gradient, feedback, right)


def right_kernel(own, left, high, low, *refs):
    *before, pieces = refs
    chips, rank, width = pieces.shape
    half = chips * width
    core, _ = position()
    side = core if own else 1 - core
    block = 512 if half % 512 == 0 else 128
    both = jnp.concatenate(split(left[...]), axis=0)
    for i in range(half // block):
        at = pl.ds(pl.multiple_of(side * half + i * block, block), block)
        total = dot(both, high[:, at], 1, 0) + dot(both, low[:, at], 1, 0)
        total = total[:rank] + total[rank:]
        start = i * block
        while start < (i + 1) * block:
            piece = start // width
            stop = min((i + 1) * block, (piece + 1) * width)
            there = (piece, slice(None), slice(start - piece * width, stop - piece * width))
            part = total[:, start - i * block : stop - i * block]
            pieces[there] = before[0][there] + part if before else part
            start = stop


def right_product(own, left, high, low, chips, width, *before):
    rank, rows = left.shape
    return pl.pallas_call(
        functools.partial(right_kernel, own),
        in_specs=[VMEM] * (3 + len(before)),
        out_specs=VMEM,
        out_shape=pltpu.VMEM((chips, rank, width), F32),
        compiler_params=params(8),
        cost_estimate=cost(8 * rows * chips * width * rank, 4 * rows * chips * width),
        name="right",
    )(left, high, low, *before)


def factor_kernel(scale, left, inverse, factor, stacked):
    rank, rows = left.shape
    values = left[...]
    gram = dot(values, values, 1, 1, HIGHEST)
    row = lax.broadcasted_iota(jnp.int32, (rank, rank), 0)
    column = lax.broadcasted_iota(jnp.int32, (rank, rank), 1)
    unit = (row == column).astype(F32)
    wide = jnp.concatenate([gram, unit], axis=1)
    row_of = lax.broadcasted_iota(jnp.int32, (rank, 1), 0)
    for j in range(rank - 1):
        pivot = wide[j : j + 1, :]
        scaled = pivot * (1.0 / pivot[:, j : j + 1])
        wide = wide - jnp.where(row_of > j, wide[:, j : j + 1], 0.0) * scaled
    diagonal = jnp.sum(wide[:, :rank] * unit, axis=1, keepdims=True)
    inv = wide[:, rank:] * (1.0 / jnp.sqrt(diagonal))
    inverse[...] = inv * scale
    q = dot(inv, values, 1, 0, HIGHEST)
    factor[...] = q
    q_high, q_low = (part.astype(F32) for part in split(q))
    stacked[...] = jnp.concatenate([q_high, q_low, q_high, q_low], axis=0).T.astype(BF16)


def factors(left, scale):
    rank, rows = left.shape
    return pl.pallas_call(
        functools.partial(factor_kernel, scale),
        in_specs=[VMEM],
        out_specs=[VMEM] * 3,
        out_shape=[
            pltpu.VMEM((rank, rank), F32),
            pltpu.VMEM((rank, rows), F32),
            pltpu.VMEM((rows, 4 * rank), BF16),
        ],
        compiler_params=params(8),
        cost_estimate=cost(2e9, 1e6),
        name="factor",
    )(left)


def feedback_kernel(own, columns, stacked, inverse, pieces, high, low, factor, feedback, right, factor_out, feedback_buf, right_buf, sems, factor_sem):
    chips, rows, width = feedback_buf.shape
    whole = high.shape[1] == columns
    core, _ = position()
    side = core if own else 1 - core
    copies = []
    if own:
        factor_copy = pltpu.make_async_copy(factor, factor_out, factor_sem)
        factor_copy.start()
    for k in range(chips):
        place = side * chips + k
        for i, start in enumerate(range(0, width, BLOCK)):
            size = min(BLOCK, width - start)
            here = pl.ds(start, size)
            at = pl.ds(pl.multiple_of(place * width + start, 128), size)
            piece = dot(inverse[...], pieces[k][:, here], 1, 0, lax.Precision.HIGH)
            right_buf[k, :, here] = piece
            piece_high, piece_low = split(piece)
            four = jnp.concatenate([piece_high, piece_high, piece_low, piece_low], axis=0)
            combined = high[:, at].astype(F32) + low[:, at].astype(F32)
            feedback_buf[k, :, here] = combined - dot(stacked[...], four, 1, 0)
            copies.append((place * width < columns, pltpu.make_async_copy(feedback_buf.at[k, :, here], feedback.at[:, at], sems.at[k, i])))
            start_or_wait(copies[-1], whole, "start")
        at = pl.ds(pl.multiple_of(place * width, 128), width)
        copies.append((place * width < columns, pltpu.make_async_copy(right_buf.at[k], right.at[:, at], sems.at[k, sems.shape[1] - 1])))
        start_or_wait(copies[-1], whole, "start")
    for copy in copies:
        start_or_wait(copy, whole, "wait")
    if own:
        factor_copy.wait()


def start_or_wait(copy, whole, action):
    inside, one = copy

    def run():
        getattr(one, action)()

    if whole:
        run()
    else:
        pl.when(inside)(run)


def new_feedback(own, stacked, inverse, given, high, low, columns, last):
    rows = high.shape[0]
    chips = sum(x.shape[0] for x in given)
    rank, width = given[0].shape[-2:]
    outs = 3 if own else 2
    first = 4 + len(given)

    def kernel(stacked, inverse, *refs):
        parts = [x.at[k] for x in refs[: len(given)] for k in range(x.shape[0])]
        if own:
            high, low, factor, feedback, right, factor_out, *scratch = refs[len(given) :]
        else:
            high, low, _, _, feedback, right, *scratch = refs[len(given) :]
            factor = factor_out = None
        feedback_kernel(own, columns, stacked, inverse, parts, high, low, factor, feedback, right, factor_out, *scratch)

    return pl.pallas_call(
        kernel,
        in_specs=[VMEM] * first + ([VMEM] if own else [ANY] * 2),
        out_specs=[ANY] * outs,
        out_shape=[
            pltpu.HBM((rows, columns), F32),
            pltpu.HBM((rank, columns), F32),
            pltpu.HBM((rank, rows), F32),
        ][:outs],
        input_output_aliases={} if own else {first: 0, first + 1: 1},
        scratch_shapes=[
            pltpu.VMEM((chips, rows, width), F32),
            pltpu.VMEM((chips, rank, width), F32),
            pltpu.SemaphoreType.DMA((chips, -(-width // BLOCK) + 1)),
            pltpu.SemaphoreType.DMA,
        ],
        compiler_params=params(16),
        cost_estimate=cost(8 * rows * chips * width * rank, 4 * rows * chips * width),
        name="feedback",
    )(stacked, inverse, *given, high, low, *last)


def swap(x, axis, mask):
    size = lax.axis_size(axis)
    return lax.ppermute(x, axis, [(i, i ^ mask) for i in range(size)])


def steps(low, high):
    return [(i, min(2, high - i)) for i in range(low, high, 2)]


def sum_stage(x, axis, low, count):
    if count == 1:
        return x + swap(x, axis, 1 << low)
    first = lax.ppermute(x, ("dp", "tensor"), pairs_of(axis, 1 << low, 3 << low))
    second = lax.ppermute(x, ("dp", "tensor"), pairs_of(axis, 1 << low, 2 << low))
    return part(x, first, second)


def pairs_of(axis, *masks):
    pairs = []
    for i in range(lax.axis_size("dp")):
        for j in range(lax.axis_size("tensor")):
            mask = masks[i % 2]
            there = (i ^ mask, j) if axis == "dp" else (i, j ^ mask)
            pairs.append(tuple(a * lax.axis_size("tensor") + b for a, b in ((i, j), there)))
    return pairs


def part_kernel(mine, first, second, out):
    core, _ = position()
    out[...] = first[...] + jnp.where(core == 1, second[...], mine[...])


def part(mine, first, second):
    return pl.pallas_call(
        part_kernel,
        in_specs=[VMEM] * 3,
        out_specs=VMEM,
        out_shape=pltpu.VMEM(mine.shape, F32),
        compiler_params=params(8),
        cost_estimate=cost(mine.size, 16 * mine.size),
        name="part",
    )(mine, first, second)


def after(x, token):
    return lax.optimization_barrier((x, token))[0]


def bits(axis):
    size = lax.axis_size(axis)
    assert size & (size - 1) == 0
    return size.bit_length() - 1


def per_device(gradient, feedback, right_factor):
    gradient, feedback = gradient[0], feedback[0]
    columns = gradient.shape[1]
    replicas = lax.axis_size("dp")
    chips = replicas // 2
    width = -(-columns // (replicas * 128)) * 128
    assert columns % width == 0

    given = [keep(x, pltpu.HBM) for x in (gradient, feedback, right_factor.T)]
    high, low, left = left_product(*given, replicas * width)
    high, low = (keep(x, pltpu.VMEM) for x in (high, low))
    left = left + swap(left, "dp", 1)
    stages = [("dp", low, count) for low, count in steps(1, bits("dp"))]
    stages += [("tensor", low, count) for low, count in steps(0, bits("tensor"))]
    stages.sort(key=lambda stage: stage[2])
    for i, stage in enumerate(stages):
        left = sum_stage(left, *stage)
        if stage[2] == 2 and i < len(stages) - 1:
            left = left + swap(left, "dp", 1)
    if stages[-1][2] == 1:
        left = left * 0.5
    beside = swap(left, "dp", 1)
    theirs, half = (right_product(side, left, high, low, chips, width) for side in (False, True))
    theirs = swap(right_product(False, beside, high, low, chips, width, theirs), "dp", 1)
    half = right_product(True, beside, high, low, chips, width, half)
    left = (left + beside) / replicas
    masks = [1 << i for i in range(1, bits("dp"))]
    parts = [half[: chips // 2] + theirs[: chips // 2], half[chips // 2 :] + theirs[chips // 2 :]]
    inverse, factor, stacked = factors(left, 1.0 / replicas**2)
    for i, pair in enumerate(zip(masks, masks[::-1])):
        came = [swap(x, "dp", mask) for x, mask in zip(parts, pair)]
        if i == 0:
            came = [after(x, inverse) for x in came]
        parts = [x + y for x, y in zip(parts, came)]

    other = swap(jnp.concatenate(parts), "dp", 1)
    *outs, factor = new_feedback(True, stacked, inverse, parts, high, low, columns, [factor])
    outs = new_feedback(False, stacked, inverse, [other], high, low, columns, outs)
    return (outs[0][None], factor.T, outs[1].T)


def solution(mesh):
    return jax.shard_map(
        per_device,
        mesh=mesh,
        in_specs=(P("dp", None, "tensor"), P("dp", None, "tensor"), P("tensor", None)),
        out_specs=(P("dp", None, "tensor"), P(), P("tensor", None)),
        check_vma=False,
    )
```

```python
import functools

import jax
import jax.numpy as jnp
from jax import lax
from jax.experimental import pallas as pl
from jax.experimental.pallas import tpu as pltpu
from jax.sharding import PartitionSpec as P

F32, BF16 = jnp.float32, jnp.bfloat16
HIGHEST = lax.Precision.HIGHEST
ANY = pl.BlockSpec(memory_space=pl.ANY)
VMEM = pl.BlockSpec(memory_space=pltpu.VMEM)


def split(x):
    high = x.astype(BF16)
    return high, (x - high.astype(F32)).astype(BF16)


def dot(a, b, a_dim, b_dim, precision=None):
    return lax.dot_general(a, b, (((a_dim,), (b_dim,)), ((), ())), precision=precision, preferred_element_type=F32)


def keep(x, space):
    return pltpu.with_memory_space_constraint(x, space)


def position():
    me = lax.axis_index("dp")
    return lax.rem(me, 2), lax.div(me, 2)


def params(mebibytes):
    return pltpu.CompilerParams(vmem_limit_bytes=mebibytes << 20)


def cost(flops, bytes_accessed):
    return pl.CostEstimate(flops=int(flops), bytes_accessed=int(bytes_accessed), transcendentals=0)


def left_kernel(chunk, gradient, feedback, right, combined, high, low, left, gradient_buf, right_buf, sems):
    rows, columns = gradient.shape
    rank = right.shape[0]
    blocks = [pl.ds(i * chunk, chunk) for i in range(columns // chunk)]
    copies = []
    for i, at in enumerate(blocks):
        group = [
            pltpu.make_async_copy(gradient.at[:, at], gradient_buf.at[:, at], sems.at[0, i]),
            pltpu.make_async_copy(feedback.at[:, at], combined.at[:, at], sems.at[1, i]),
            pltpu.make_async_copy(right.at[:, at], right_buf.at[:, at], sems.at[2, i]),
        ]
        for copy in group:
            copy.start()
        copies.append(group)
    padded = combined.shape[1]
    if padded > columns:
        rest = pl.ds(columns, padded - columns)
        combined[:, rest] = jnp.zeros((rows, padded - columns), F32)
        high[:, rest] = jnp.zeros((rows, padded - columns), BF16)
        low[:, rest] = jnp.zeros((rows, padded - columns), BF16)
    total = jnp.zeros((rows, 2 * rank), F32)
    for at, group in zip(blocks, copies):
        for copy in group:
            copy.wait()
        both = jnp.concatenate(split(right_buf[:, at]), axis=0)
        c = combined[:, at] + gradient_buf[:, at].astype(F32)
        c_high, c_low = split(c)
        combined[:, at] = c
        high[:, at] = c_high
        low[:, at] = c_low
        total += dot(c_high, both, 1, 1) + dot(c_low, both, 1, 1)
    left[...] = (total[:, :rank] + total[:, rank:]).T


def left_product(gradient, feedback, right, padded):
    rows, columns = gradient.shape
    rank = right.shape[0]
    chunk = next(c for c in (1024, 512, 128) if columns % c == 0)
    return pl.pallas_call(
        functools.partial(left_kernel, chunk),
        in_specs=[ANY] * 3,
        out_specs=[VMEM] * 4,
        out_shape=[
            pltpu.VMEM((rows, padded), F32),
            pltpu.VMEM((rows, padded), BF16),
            pltpu.VMEM((rows, padded), BF16),
            pltpu.VMEM((rank, rows), F32),
        ],
        scratch_shapes=[
            pltpu.VMEM((rows, columns), BF16),
            pltpu.VMEM((rank, columns), F32),
            pltpu.SemaphoreType.DMA((3, columns // chunk)),
        ],
        compiler_params=params(16),
        cost_estimate=cost(8 * rows * columns * rank, 6 * rows * columns),
        name="left",
    )(gradient, feedback, right)


def right_kernel(own, left, high, low, *refs):
    *before, pieces = refs
    chips, rank, width = pieces.shape
    half = chips * width
    core, _ = position()
    side = core if own else 1 - core
    block = 512 if half % 512 == 0 else 128
    both = jnp.concatenate(split(left[...]), axis=0)
    for i in range(half // block):
        at = pl.ds(pl.multiple_of(side * half + i * block, block), block)
        total = dot(both, high[:, at], 1, 0) + dot(both, low[:, at], 1, 0)
        total = total[:rank] + total[rank:]
        start = i * block
        while start < (i + 1) * block:
            piece = start // width
            stop = min((i + 1) * block, (piece + 1) * width)
            there = (piece, slice(None), slice(start - piece * width, stop - piece * width))
            part = total[:, start - i * block : stop - i * block]
            pieces[there] = before[0][there] + part if before else part
            start = stop


def right_product(own, left, high, low, chips, width, *before):
    rank, rows = left.shape
    return pl.pallas_call(
        functools.partial(right_kernel, own),
        in_specs=[VMEM] * (3 + len(before)),
        out_specs=VMEM,
        out_shape=pltpu.VMEM((chips, rank, width), F32),
        compiler_params=params(8),
        cost_estimate=cost(8 * rows * chips * width * rank, 4 * rows * chips * width),
        name="right",
    )(left, high, low, *before)


def factor_kernel(scale, left, inverse, factor, stacked):
    rank, rows = left.shape
    values = left[...]
    gram = dot(values, values, 1, 1, HIGHEST)
    row = lax.broadcasted_iota(jnp.int32, (rank, rank), 0)
    column = lax.broadcasted_iota(jnp.int32, (rank, rank), 1)
    unit = (row == column).astype(F32)
    wide = jnp.concatenate([gram, unit], axis=1)
    row_of = lax.broadcasted_iota(jnp.int32, (rank, 1), 0)
    for j in range(rank - 1):
        pivot = wide[j : j + 1, :]
        scaled = pivot * (1.0 / pivot[:, j : j + 1])
        wide = wide - jnp.where(row_of > j, wide[:, j : j + 1], 0.0) * scaled
    diagonal = jnp.sum(wide[:, :rank] * unit, axis=1, keepdims=True)
    inv = wide[:, rank:] * (1.0 / jnp.sqrt(diagonal))
    inverse[...] = inv * scale
    q = dot(inv, values, 1, 0, HIGHEST)
    factor[...] = q
    q_high, q_low = (part.astype(F32) for part in split(q))
    stacked[...] = jnp.concatenate([q_high, q_low, q_high, q_low], axis=0).T.astype(BF16)


def factors(left, scale):
    rank, rows = left.shape
    return pl.pallas_call(
        functools.partial(factor_kernel, scale),
        in_specs=[VMEM],
        out_specs=[VMEM] * 3,
        out_shape=[
            pltpu.VMEM((rank, rank), F32),
            pltpu.VMEM((rank, rows), F32),
            pltpu.VMEM((rows, 4 * rank), BF16),
        ],
        compiler_params=params(8),
        cost_estimate=cost(2e9, 1e6),
        name="factor",
    )(left)


def feedback_kernel(own, columns, stacked, inverse, pieces, combined, factor, feedback, right, factor_out, feedback_buf, right_buf, sems, factor_sem):
    chips, rows, width = feedback_buf.shape
    whole = combined.shape[1] == columns
    core, _ = position()
    side = core if own else 1 - core
    copies = []
    if own:
        factor_copy = pltpu.make_async_copy(factor, factor_out, factor_sem)
        factor_copy.start()
    rights = [dot(inverse[...], pieces[k][...], 1, 0, lax.Precision.HIGH) for k in range(chips)]
    for k, piece in enumerate(rights):
        right_buf[k] = piece
    for k, piece in enumerate(rights):
        place = side * chips + k
        at = pl.ds(pl.multiple_of(place * width, 128), width)
        piece_high, piece_low = split(piece)
        four = jnp.concatenate([piece_high, piece_high, piece_low, piece_low], axis=0)
        feedback_buf[k] = combined[:, at] - dot(stacked[...], four, 1, 0)
        copies.append(
            (
                place * width < columns,
                pltpu.make_async_copy(feedback_buf.at[k], feedback.at[:, at], sems.at[0, k]),
                pltpu.make_async_copy(right_buf.at[k], right.at[:, at], sems.at[1, k]),
            )
        )
        start_or_wait(copies[-1], whole, "start")
    for copy in copies:
        start_or_wait(copy, whole, "wait")
    if own:
        factor_copy.wait()


def start_or_wait(copy, whole, action):
    inside, *both = copy

    def run():
        for one in both:
            getattr(one, action)()

    if whole:
        run()
    else:
        pl.when(inside)(run)


def new_feedback(own, stacked, inverse, given, combined, columns, last):
    rows = combined.shape[0]
    chips = sum(x.shape[0] for x in given)
    rank, width = given[0].shape[-2:]
    outs = 3 if own else 2
    first = 3 + len(given)

    def kernel(stacked, inverse, *refs):
        parts = [x.at[k] for x in refs[: len(given)] for k in range(x.shape[0])]
        if own:
            combined, factor, feedback, right, factor_out, *scratch = refs[len(given) :]
        else:
            combined, _, _, feedback, right, *scratch = refs[len(given) :]
            factor = factor_out = None
        feedback_kernel(own, columns, stacked, inverse, parts, combined, factor, feedback, right, factor_out, *scratch)

    return pl.pallas_call(
        kernel,
        in_specs=[VMEM] * first + ([VMEM] if own else [ANY] * 2),
        out_specs=[ANY] * outs,
        out_shape=[
            pltpu.HBM((rows, columns), F32),
            pltpu.HBM((rank, columns), F32),
            pltpu.HBM((rank, rows), F32),
        ][:outs],
        input_output_aliases={} if own else {first: 0, first + 1: 1},
        scratch_shapes=[
            pltpu.VMEM((chips, rows, width), F32),
            pltpu.VMEM((chips, rank, width), F32),
            pltpu.SemaphoreType.DMA((2, chips)),
            pltpu.SemaphoreType.DMA,
        ],
        compiler_params=params(16),
        cost_estimate=cost(8 * rows * chips * width * rank, 4 * rows * chips * width),
        name="feedback",
    )(stacked, inverse, *given, combined, *last)


def swap(x, axis, mask):
    size = lax.axis_size(axis)
    return lax.ppermute(x, axis, [(i, i ^ mask) for i in range(size)])


def steps(low, high):
    return [(i, min(2, high - i)) for i in range(low, high, 2)]


def sum_stage(x, axis, low, count):
    if count == 1:
        return x + swap(x, axis, 1 << low)
    first = lax.ppermute(x, ("dp", "tensor"), pairs_of(axis, 1 << low, 3 << low))
    second = lax.ppermute(x, ("dp", "tensor"), pairs_of(axis, 1 << low, 2 << low))
    return part(x, first, second)


def pairs_of(axis, *masks):
    pairs = []
    for i in range(lax.axis_size("dp")):
        for j in range(lax.axis_size("tensor")):
            mask = masks[i % 2]
            there = (i ^ mask, j) if axis == "dp" else (i, j ^ mask)
            pairs.append(tuple(a * lax.axis_size("tensor") + b for a, b in ((i, j), there)))
    return pairs


def part_kernel(mine, first, second, out):
    core, _ = position()
    out[...] = first[...] + jnp.where(core == 1, second[...], mine[...])


def part(mine, first, second):
    return pl.pallas_call(
        part_kernel,
        in_specs=[VMEM] * 3,
        out_specs=VMEM,
        out_shape=pltpu.VMEM(mine.shape, F32),
        compiler_params=params(8),
        cost_estimate=cost(mine.size, 16 * mine.size),
        name="part",
    )(mine, first, second)


def after(x, token):
    return lax.optimization_barrier((x, token))[0]


def bits(axis):
    size = lax.axis_size(axis)
    assert size & (size - 1) == 0
    return size.bit_length() - 1


def per_device(gradient, feedback, right_factor):
    gradient, feedback = gradient[0], feedback[0]
    columns = gradient.shape[1]
    replicas = lax.axis_size("dp")
    chips = replicas // 2
    width = -(-columns // (replicas * 128)) * 128
    assert columns % width == 0

    given = [keep(x, pltpu.HBM) for x in (gradient, feedback, right_factor.T)]
    combined, high, low, left = left_product(*given, replicas * width)
    combined, high, low = (keep(x, pltpu.VMEM) for x in (combined, high, low))
    left = left + swap(left, "dp", 1)
    stages = [("dp", low, count) for low, count in steps(1, bits("dp"))]
    stages += [("tensor", low, count) for low, count in steps(0, bits("tensor"))]
    stages.sort(key=lambda stage: stage[2])
    for i, stage in enumerate(stages):
        left = sum_stage(left, *stage)
        if stage[2] == 2 and i < len(stages) - 1:
            left = left + swap(left, "dp", 1)
    if stages[-1][2] == 1:
        left = left * 0.5
    beside = swap(left, "dp", 1)
    theirs, half = (right_product(side, left, high, low, chips, width) for side in (False, True))
    theirs = swap(right_product(False, beside, high, low, chips, width, theirs), "dp", 1)
    half = right_product(True, beside, high, low, chips, width, half)
    left = (left + beside) / replicas
    masks = [1 << i for i in range(1, bits("dp"))]
    parts = [half[: chips // 2] + theirs[: chips // 2], half[chips // 2 :] + theirs[chips // 2 :]]
    inverse, factor, stacked = factors(left, 1.0 / replicas**2)
    for i, pair in enumerate(zip(masks, masks[::-1])):
        came = [swap(x, "dp", mask) for x, mask in zip(parts, pair)]
        if i == 0:
            came = [after(x, inverse) for x in came]
        parts = [x + y for x, y in zip(parts, came)]

    other = swap(jnp.concatenate(parts), "dp", 1)
    *outs, factor = new_feedback(True, stacked, inverse, parts, combined, columns, [factor])
    outs = new_feedback(False, stacked, inverse, [other], combined, columns, outs)
    return (outs[0][None], factor.T, outs[1].T)


def solution(mesh):
    return jax.shard_map(
        per_device,
        mesh=mesh,
        in_specs=(P("dp", None, "tensor"), P("dp", None, "tensor"), P("tensor", None)),
        out_specs=(P("dp", None, "tensor"), P(), P("tensor", None)),
        check_vma=False,
    )
```

```python
import functools

import jax
import jax.numpy as jnp
from jax import lax
from jax.experimental import pallas as pl
from jax.experimental.pallas import tpu as pltpu
from jax.sharding import PartitionSpec as P

F32, BF16 = jnp.float32, jnp.bfloat16
HIGHEST = lax.Precision.HIGHEST
ANY = pl.BlockSpec(memory_space=pl.ANY)
VMEM = pl.BlockSpec(memory_space=pltpu.VMEM)


def split(x):
    high = x.astype(BF16)
    return high, (x - high.astype(F32)).astype(BF16)


def dot(a, b, a_dim, b_dim, precision=None):
    return lax.dot_general(a, b, (((a_dim,), (b_dim,)), ((), ())), precision=precision, preferred_element_type=F32)


def keep(x, space):
    return pltpu.with_memory_space_constraint(x, space)


def position():
    me = lax.axis_index("dp")
    return lax.rem(me, 2), lax.div(me, 2)


def params(mebibytes):
    return pltpu.CompilerParams(vmem_limit_bytes=mebibytes << 20)


def cost(flops, bytes_accessed):
    return pl.CostEstimate(flops=int(flops), bytes_accessed=int(bytes_accessed), transcendentals=0)


def left_kernel(chunk, gradient, feedback, right, combined, high, low, left, gradient_buf, right_buf, sems):
    rows, columns = gradient.shape
    rank = right.shape[0]
    blocks = [pl.ds(i * chunk, chunk) for i in range(columns // chunk)]
    copies = []
    for i, at in enumerate(blocks):
        group = [
            pltpu.make_async_copy(gradient.at[:, at], gradient_buf.at[:, at], sems.at[0, i]),
            pltpu.make_async_copy(feedback.at[:, at], combined.at[:, at], sems.at[1, i]),
            pltpu.make_async_copy(right.at[:, at], right_buf.at[:, at], sems.at[2, i]),
        ]
        for copy in group:
            copy.start()
        copies.append(group)
    padded = combined.shape[1]
    if padded > columns:
        rest = pl.ds(columns, padded - columns)
        combined[:, rest] = jnp.zeros((rows, padded - columns), F32)
        high[:, rest] = jnp.zeros((rows, padded - columns), BF16)
        low[:, rest] = jnp.zeros((rows, padded - columns), BF16)
    total = jnp.zeros((rows, 2 * rank), F32)
    for at, group in zip(blocks, copies):
        for copy in group:
            copy.wait()
        both = jnp.concatenate(split(right_buf[:, at]), axis=0)
        c = combined[:, at] + gradient_buf[:, at].astype(F32)
        c_high, c_low = split(c)
        combined[:, at] = c
        high[:, at] = c_high
        low[:, at] = c_low
        total += dot(c_high, both, 1, 1) + dot(c_low, both, 1, 1)
    left[...] = (total[:, :rank] + total[:, rank:]).T


def left_product(gradient, feedback, right, padded):
    rows, columns = gradient.shape
    rank = right.shape[0]
    chunk = next(c for c in (1024, 512, 128) if columns % c == 0)
    return pl.pallas_call(
        functools.partial(left_kernel, chunk),
        in_specs=[ANY] * 3,
        out_specs=[VMEM] * 4,
        out_shape=[
            pltpu.VMEM((rows, padded), F32),
            pltpu.VMEM((rows, padded), BF16),
            pltpu.VMEM((rows, padded), BF16),
            pltpu.VMEM((rank, rows), F32),
        ],
        scratch_shapes=[
            pltpu.VMEM((rows, columns), BF16),
            pltpu.VMEM((rank, columns), F32),
            pltpu.SemaphoreType.DMA((3, columns // chunk)),
        ],
        compiler_params=params(16),
        cost_estimate=cost(8 * rows * columns * rank, 6 * rows * columns),
        name="left",
    )(gradient, feedback, right)


def right_kernel(own, left, high, low, *refs):
    *before, pieces = refs
    chips, rank, width = pieces.shape
    half = chips * width
    core, _ = position()
    side = core if own else 1 - core
    block = 512 if half % 512 == 0 else 128
    both = jnp.concatenate(split(left[...]), axis=0)
    for i in range(half // block):
        at = pl.ds(pl.multiple_of(side * half + i * block, block), block)
        total = dot(both, high[:, at], 1, 0) + dot(both, low[:, at], 1, 0)
        total = total[:rank] + total[rank:]
        start = i * block
        while start < (i + 1) * block:
            piece = start // width
            stop = min((i + 1) * block, (piece + 1) * width)
            there = (piece, slice(None), slice(start - piece * width, stop - piece * width))
            part = total[:, start - i * block : stop - i * block]
            pieces[there] = before[0][there] + part if before else part
            start = stop


def right_product(own, left, high, low, chips, width, *before):
    rank, rows = left.shape
    return pl.pallas_call(
        functools.partial(right_kernel, own),
        in_specs=[VMEM] * (3 + len(before)),
        out_specs=VMEM,
        out_shape=pltpu.VMEM((chips, rank, width), F32),
        compiler_params=params(8),
        cost_estimate=cost(8 * rows * chips * width * rank, 4 * rows * chips * width),
        name="right",
    )(left, high, low, *before)


def factor_kernel(scale, left, inverse, factor, stacked):
    rank, rows = left.shape
    values = left[...]
    gram = dot(values, values, 1, 1, HIGHEST)
    row = lax.broadcasted_iota(jnp.int32, (rank, rank), 0)
    column = lax.broadcasted_iota(jnp.int32, (rank, rank), 1)
    unit = (row == column).astype(F32)
    wide = jnp.concatenate([gram, unit], axis=1)
    row_of = lax.broadcasted_iota(jnp.int32, (rank, 1), 0)
    for j in range(rank - 1):
        pivot = wide[j : j + 1, :]
        scaled = pivot * (1.0 / pivot[:, j : j + 1])
        wide = wide - jnp.where(row_of > j, wide[:, j : j + 1], 0.0) * scaled
    diagonal = jnp.sum(wide[:, :rank] * unit, axis=1, keepdims=True)
    inv = wide[:, rank:] * (1.0 / jnp.sqrt(diagonal))
    inverse[...] = inv * scale
    q = dot(inv, values, 1, 0, HIGHEST)
    factor[...] = q
    q_high, q_low = (part.astype(F32) for part in split(q))
    stacked[...] = jnp.concatenate([q_high, q_low, q_high, q_low], axis=0).T.astype(BF16)


def factors(left, scale):
    rank, rows = left.shape
    return pl.pallas_call(
        functools.partial(factor_kernel, scale),
        in_specs=[VMEM],
        out_specs=[VMEM] * 3,
        out_shape=[
            pltpu.VMEM((rank, rank), F32),
            pltpu.VMEM((rank, rows), F32),
            pltpu.VMEM((rows, 4 * rank), BF16),
        ],
        compiler_params=params(8),
        cost_estimate=cost(2e9, 1e6),
        name="factor",
    )(left)


def feedback_kernel(own, columns, stacked, inverse, pieces, combined, factor, feedback, right, factor_out, feedback_buf, right_buf, sems, factor_sem):
    chips, rows, width = feedback_buf.shape
    whole = combined.shape[1] == columns
    core, _ = position()
    side = core if own else 1 - core
    copies = []
    if own:
        factor_copy = pltpu.make_async_copy(factor, factor_out, factor_sem)
        factor_copy.start()
    rights = [dot(inverse[...], pieces[k][...], 1, 0, lax.Precision.HIGH) for k in range(chips)]
    for k, piece in enumerate(rights):
        right_buf[k] = piece
    for k, piece in enumerate(rights):
        place = side * chips + k
        at = pl.ds(pl.multiple_of(place * width, 128), width)
        piece_high, piece_low = split(piece)
        four = jnp.concatenate([piece_high, piece_high, piece_low, piece_low], axis=0)
        feedback_buf[k] = combined[:, at] - dot(stacked[...], four, 1, 0)
        copies.append(
            (
                place * width < columns,
                pltpu.make_async_copy(feedback_buf.at[k], feedback.at[:, at], sems.at[0, k]),
                pltpu.make_async_copy(right_buf.at[k], right.at[:, at], sems.at[1, k]),
            )
        )
        start_or_wait(copies[-1], whole, "start")
    for copy in copies:
        start_or_wait(copy, whole, "wait")
    if own:
        factor_copy.wait()


def start_or_wait(copy, whole, action):
    inside, *both = copy

    def run():
        for one in both:
            getattr(one, action)()

    if whole:
        run()
    else:
        pl.when(inside)(run)


def new_feedback(own, stacked, inverse, given, combined, columns, last):
    rows = combined.shape[0]
    chips = sum(x.shape[0] for x in given)
    rank, width = given[0].shape[-2:]
    outs = 3 if own else 2
    first = 3 + len(given)

    def kernel(stacked, inverse, *refs):
        parts = [x.at[k] for x in refs[: len(given)] for k in range(x.shape[0])]
        if own:
            combined, factor, feedback, right, factor_out, *scratch = refs[len(given) :]
        else:
            combined, _, _, feedback, right, *scratch = refs[len(given) :]
            factor = factor_out = None
        feedback_kernel(own, columns, stacked, inverse, parts, combined, factor, feedback, right, factor_out, *scratch)

    return pl.pallas_call(
        kernel,
        in_specs=[VMEM] * first + ([VMEM] if own else [ANY] * 2),
        out_specs=[ANY] * outs,
        out_shape=[
            pltpu.HBM((rows, columns), F32),
            pltpu.HBM((rank, columns), F32),
            pltpu.HBM((rank, rows), F32),
        ][:outs],
        input_output_aliases={} if own else {first: 0, first + 1: 1},
        scratch_shapes=[
            pltpu.VMEM((chips, rows, width), F32),
            pltpu.VMEM((chips, rank, width), F32),
            pltpu.SemaphoreType.DMA((2, chips)),
            pltpu.SemaphoreType.DMA,
        ],
        compiler_params=params(16),
        cost_estimate=cost(8 * rows * chips * width * rank, 4 * rows * chips * width),
        name="feedback",
    )(stacked, inverse, *given, combined, *last)


def swap(x, axis, mask):
    size = lax.axis_size(axis)
    return lax.ppermute(x, axis, [(i, i ^ mask) for i in range(size)])


def steps(low, high):
    return [(i, min(2, high - i)) for i in range(low, high, 2)]


def sum_stage(x, axis, low, count):
    if count == 1:
        return x + swap(x, axis, 1 << low)
    first = lax.ppermute(x, ("dp", "tensor"), pairs_of(axis, 1 << low, 3 << low))
    second = lax.ppermute(x, ("dp", "tensor"), pairs_of(axis, 1 << low, 2 << low))
    return part(x, first, second)


def pairs_of(axis, *masks):
    pairs = []
    for i in range(lax.axis_size("dp")):
        for j in range(lax.axis_size("tensor")):
            mask = masks[i % 2]
            there = (i ^ mask, j) if axis == "dp" else (i, j ^ mask)
            pairs.append(tuple(a * lax.axis_size("tensor") + b for a, b in ((i, j), there)))
    return pairs


def part_kernel(mine, first, second, out):
    core, _ = position()
    out[...] = first[...] + jnp.where(core == 1, second[...], mine[...])


def part(mine, first, second):
    return pl.pallas_call(
        part_kernel,
        in_specs=[VMEM] * 3,
        out_specs=VMEM,
        out_shape=pltpu.VMEM(mine.shape, F32),
        compiler_params=params(8),
        cost_estimate=cost(mine.size, 16 * mine.size),
        name="part",
    )(mine, first, second)


def after(x, token):
    return lax.optimization_barrier((x, token))[0]


def bits(axis):
    size = lax.axis_size(axis)
    assert size & (size - 1) == 0
    return size.bit_length() - 1


def per_device(gradient, feedback, right_factor):
    gradient, feedback = gradient[0], feedback[0]
    columns = gradient.shape[1]
    replicas = lax.axis_size("dp")
    chips = replicas // 2
    width = -(-columns // (replicas * 128)) * 128
    assert columns % width == 0

    given = [keep(x, pltpu.HBM) for x in (gradient, feedback, right_factor.T)]
    combined, high, low, left = left_product(*given, replicas * width)
    combined, high, low = (keep(x, pltpu.VMEM) for x in (combined, high, low))
    left = left + swap(left, "dp", 1)
    stages = [("dp", low, count) for low, count in steps(1, bits("dp"))]
    stages += [("tensor", low, count) for low, count in steps(0, bits("tensor"))]
    stages.sort(key=lambda stage: stage[2])
    for i, stage in enumerate(stages):
        left = sum_stage(left, *stage)
        if stage[2] == 2 and i < len(stages) - 1:
            left = left + swap(left, "dp", 1)
    if stages[-1][2] == 1:
        left = left * 0.5
    beside = swap(left, "dp", 1)
    theirs, half = (right_product(side, left, high, low, chips, width) for side in (False, True))
    theirs = swap(right_product(False, beside, high, low, chips, width, theirs), "dp", 1)
    half = right_product(True, beside, high, low, chips, width, half)
    left = (left + beside) / replicas
    masks = [1 << i for i in range(1, bits("dp"))]
    parts = [half[: chips // 2] + theirs[: chips // 2], half[chips // 2 :] + theirs[chips // 2 :]]
    inverse, factor, stacked = factors(left, 1.0 / replicas**2)
    for i, pair in enumerate(zip(masks, masks[::-1])):
        came = [lax.ppermute(x, ("dp", "tensor"), pairs_of("dp", *order)) for x, order in zip(parts, (pair, pair[::-1]))]
        if i == 0:
            came = [after(x, inverse) for x in came]
        parts = [x + y for x, y in zip(parts, came)]

    other = swap(jnp.concatenate(parts), "dp", 1)
    *outs, factor = new_feedback(True, stacked, inverse, parts, combined, columns, [factor])
    outs = new_feedback(False, stacked, inverse, [other], combined, columns, outs)
    return (outs[0][None], factor.T, outs[1].T)


def solution(mesh):
    return jax.shard_map(
        per_device,
        mesh=mesh,
        in_specs=(P("dp", None, "tensor"), P("dp", None, "tensor"), P("tensor", None)),
        out_specs=(P("dp", None, "tensor"), P(), P("tensor", None)),
        check_vma=False,
    )
```
